32 devices in a mesh: group: 2 (over x), dp: 2 (over core), expert: 8 (over z, y).
Axes of the slice: x: 2, y: 2, z: 4, core: 2. Of those that a mesh axis runs over, the one named last changes fastest.
Arguments:
- layer_input: bfloat16 [2, 128, 4096], P(None, ('group', 'dp', 'expert')), parts along dimension 1, may hold values from -6 to 6
- prompt_ssm: float32 [8, 16, 4096], P(('group', 'dp'), None, 'expert'), parts along dimension 0, may hold values from -4 to 4
- prompt_conv: float32 [8, 3, 4096], P(('group', 'dp'), None, 'expert'), parts along dimension 0, may hold values from -6 to 6
- sample_prompt: int32 [128], P(('group', 'dp')), parts along dimension 0, may hold values from 0 to 3, as said below
- mamba_gain: float32 [4096], replicated, may hold values from 0.25 to 1.75
- in_proj: bfloat16 [2, 4096, 4096], P(None, None, 'expert'), may hold values from -0.09375 to 0.09375
- conv_weight: float32 [4, 4096], P(None, 'expert'), may hold values from -3 to 3
- conv_bias: float32 [4096], P('expert'), may hold values from -3 to 3
- x_proj: bfloat16 [288, 4096], P(None, 'expert'), may hold values from -0.09375 to 0.09375
- dt_proj: bfloat16 [256, 4096], P(None, 'expert'), may hold values from -0.375 to 0.375
- dt_bias: float32 [4096], P('expert'), may hold values from -4 to -1
- a_log: float32 [16, 4096], P(None, 'expert'), may hold values from -3 to 2
- d_skip: float32 [4096], P('expert'), may hold values from 0.5 to 1.5
- out_proj: bfloat16 [4096, 4096], P('expert'), may hold values from -0.09375 to 0.09375
- moe_gain: float32 [4096], replicated, may hold values from 0.1 to 1.9
- route_ids: int32 [2, 128, 2], P(None, ('group', 'dp', 'expert')), parts along dimension 1, may hold values from 0 to 15, as said below
- route_weights: float32 [2, 128, 2], P(None, ('group', 'dp', 'expert')), parts along dimension 1, may hold values from 0.2 to 0.9
- w_gate: bfloat16 [2, 7168, 4096], P('dp', 'expert'), may hold values from -0.09375 to 0.09375
- w_up: bfloat16 [2, 7168, 4096], P('dp', 'expert'), may hold values from -0.09375 to 0.09375
- w_down: bfloat16 [2, 7168, 4096], P('dp', 'expert'), may hold values from -0.0625 to 0.0625
Outputs:
- layer_output: bfloat16 [2, 128, 4096], P(None, ('group', 'dp', 'expert')), parts along dimension 1
- ssm_state: float32 [128, 16, 4096], P(('group', 'dp'), None, 'expert'), parts along dimension 0
- conv_state: float32 [128, 3, 4096], P(('group', 'dp'), None, 'expert'), parts along dimension 0
The draws below stay inside these ranges and needn't reach their ends.
There are 2 independent parts, one for each index of `group`. The reference program is written for one: setup_inputs(seed, part) draws one part's arguments, and reference() takes and returns one part's arrays. A program takes and returns all parts, laid end to end along the dimension named above; an argument that names none is the same for every part. Nothing has to cross between parts.
Inputs may be any that keep to these rules, and one draw needn't show every extreme that they name: `sample_prompt`: each prompt is the prompt of exactly 16 rows. `route_ids`: each row names 2 different experts; in each step and each aligned block of 4 rows (the rows of one device) at most 2 rows name a given expert below 2, and in every step some expert below 2 is named by exactly 2 rows in every block.
All inputs are finite; a program needn't handle non-finite values.
Results may differ from the reference program's by a relative error of at most 0.014.
Values may be sent and summed in bfloat16 or wider, within the bound.
No kernel may reach another device: no remote copies, remote signals or barrier semaphores. Data moves between devices by JAX's collectives and lax.ppermute only.
A program may use at most 128 MiB of HBM per device.

```python
import jax
import jax.numpy as jnp
from jax import lax

D = 4096
INNER = 4096
NS = 16
DTR = 256
KC = 4
FFW = 7168
EXPERTS = 16
TOPK = 2
GROUP = 16
STEPS = 2
CAP = 2
ROWS_DEV = 4
EW = 2
ROWS = 64
PROMPTS = 4
PROJ = 288
N_DP = 2
N_EXPERT = 8


def draw_sample_prompt(key, part):
    key = jax.random.fold_in(key, 5)
    order = jax.random.permutation(key, ROWS)
    return (order // GROUP).astype(jnp.int32)


def draw_route_ids(key, part):
    key = jax.random.fold_in(key, 11)
    blocks = N_DP * N_EXPERT
    keys = jax.random.split(key, 6)
    hottest = jax.random.randint(keys[0], (STEPS, 1, 1), 0, EW)
    counts = jax.random.randint(keys[1], (STEPS, blocks, EW), 0, CAP + 1)
    which = jnp.arange(EW)[None, None, :]
    counts = jnp.where(which == hottest, CAP, counts)
    scores = jax.random.randint(keys[2], (STEPS, blocks, EW, ROWS_DEV), 0, 1 << 20) * ROWS_DEV + jnp.arange(ROWS_DEV)
    ranks = jnp.argsort(jnp.argsort(scores, axis=-1), axis=-1)
    member = ranks < counts[..., None]
    first_in = member[:, :, 0, :]
    second_in = member[:, :, 1, :]
    spare = EXPERTS - EW
    other_a = EW + jax.random.randint(keys[3], (STEPS, blocks, ROWS_DEV), 0, spare)
    other_b = EW + (other_a - EW + 1 + jax.random.randint(keys[4], (STEPS, blocks, ROWS_DEV), 0, spare - 1)) % spare
    leading = jnp.where(first_in, 0, jnp.where(second_in, 1, other_a))
    trailing = jnp.where(first_in & second_in, 1, jnp.where(first_in | second_in, other_a, other_b))
    paired = jnp.stack([leading, trailing], axis=-1)
    flipped = jax.random.randint(keys[5], (STEPS, blocks, ROWS_DEV), 0, 2)
    paired = jnp.where(flipped[..., None] == 1, paired[..., ::-1], paired)
    return paired.reshape(STEPS, ROWS, TOPK).astype(jnp.int32)


def level_of(key, dims, pieces, low, top_value):
    def one(position, blocks):
        steps = jax.random.uniform(jax.random.fold_in(jax.random.fold_in(key, 6), position), (blocks,), jnp.float32, low / len(pieces), top_value / len(pieces))
        return jnp.repeat(jnp.exp(steps), dims[position] // blocks).reshape((-1,) + (1,) * (len(dims) - position - 1))

    factor_of = one(*pieces[0])
    for cut in pieces[1:]:
        factor_of = factor_of * one(*cut)
    return factor_of


def noise(stream_key, dims, spread, bound, cuts=(), held_as=jnp.bfloat16):
    entries = spread * jax.random.normal(stream_key, dims, jnp.float32)
    if cuts:
        entries = entries * level_of(stream_key, dims, cuts, -0.22, 0.18)
    return jnp.clip(entries, -bound, bound).astype(held_as)


def setup_inputs(seed: int = 0, part: int = 0) -> dict:
    arg_keys = jax.random.split(jax.random.key(seed), 21)
    own_keys = jax.random.split(jax.random.fold_in(arg_keys[20], part), 21)
    return {
        "layer_input": noise(own_keys[0], (STEPS, ROWS, D), 1.0, 6.0, ((1, 16),)),
        "prompt_ssm": noise(own_keys[1], (PROMPTS, NS, INNER), 0.5, 4.0, ((0, 2), (2, 8)), jnp.float32),
        "prompt_conv": noise(own_keys[2], (PROMPTS, KC - 1, INNER), 1.0, 6.0, ((0, 2), (2, 8)), jnp.float32),
        "sample_prompt": draw_sample_prompt(jax.random.fold_in(jax.random.fold_in(arg_keys[20], part), 71), part),
        "mamba_gain": jnp.clip(1.0 + 0.15 * jax.random.normal(arg_keys[4], (D,), jnp.float32), 0.25, 1.75),
        "in_proj": noise(arg_keys[5], (2, D, INNER), D ** -0.5, 0.09375, ((2, 8),)),
        "conv_weight": noise(arg_keys[6], (KC, INNER), KC ** -0.5, 3.0, ((1, 8),), jnp.float32),
        "conv_bias": noise(arg_keys[7], (INNER,), 0.5, 3.0, ((0, 8),), jnp.float32),
        "x_proj": noise(arg_keys[8], (PROJ, INNER), INNER ** -0.5, 0.09375, ((1, 8),)),
        "dt_proj": noise(arg_keys[9], (DTR, INNER), DTR ** -0.5, 0.375, ((1, 8),)),
        "dt_bias": jnp.clip(-4.0 + 3.0 * jax.random.uniform(arg_keys[10], (INNER,), jnp.float32) ** level_of(arg_keys[10], (INNER,), ((0, 8),), -0.2, 0.2), -4.0, -1.0),
        "a_log": jnp.clip(-3.0 + 5.0 * jax.random.uniform(arg_keys[11], (NS, INNER), jnp.float32) ** level_of(arg_keys[11], (NS, INNER), ((1, 8),), -0.2, 0.2), -3.0, 2.0),
        "d_skip": jnp.clip(0.5 + 1.0 * jax.random.uniform(arg_keys[12], (INNER,), jnp.float32) ** level_of(arg_keys[12], (INNER,), ((0, 8),), -0.2, 0.2), 0.5, 1.5),
        "out_proj": noise(arg_keys[13], (INNER, D), INNER ** -0.5, 0.09375, ((0, 8),)),
        "moe_gain": jnp.clip(1.0 + 0.18 * jax.random.normal(arg_keys[14], (D,), jnp.float32), 0.1, 1.9),
        "route_ids": draw_route_ids(jax.random.fold_in(jax.random.fold_in(arg_keys[20], part), 71), part),
        "route_weights": jnp.clip(0.2 + 0.7 * jax.random.uniform(own_keys[16], (STEPS, ROWS, TOPK), jnp.float32) ** level_of(own_keys[16], (STEPS, ROWS, TOPK), ((1, 16),), -0.2, 0.2), 0.2, 0.9),
        "w_gate": noise(arg_keys[17], (EW, FFW, D), D ** -0.5, 0.09375, ((0, 2), (1, 8))),
        "w_up": noise(arg_keys[18], (EW, FFW, D), D ** -0.5, 0.09375, ((0, 2), (1, 8))),
        "w_down": noise(arg_keys[19], (EW, FFW, D), FFW ** -0.5, 0.0625, ((0, 2), (1, 8))),
    }


def normalize(values, gain):
    return values * lax.rsqrt(lax.optimization_barrier(jnp.mean(values * values, axis=-1, keepdims=True)) + 1e-05) * gain

def reference(layer_input, prompt_ssm, prompt_conv, sample_prompt, mamba_gain, in_proj, conv_weight, conv_bias, x_proj, dt_proj, dt_bias, a_log, d_skip, out_proj, moe_gain, route_ids, route_weights, w_gate, w_up, w_down):
    ssm_state = prompt_ssm[sample_prompt]
    conv_state = prompt_conv[sample_prompt]
    decay_rate = -jnp.exp(a_log)
    outputs = []
    for step_index in range(STEPS):
        inputs = layer_input[step_index].astype(jnp.float32)
        if step_index > 0:
            inputs = outputs[-1].astype(jnp.float32) + inputs
        normed = normalize(inputs, mamba_gain).astype(jnp.bfloat16)
        x_part = jnp.dot(normed, in_proj[0], preferred_element_type=jnp.float32)
        z_part = jnp.dot(normed, in_proj[1], preferred_element_type=jnp.float32)
        window = jnp.concatenate([conv_state, x_part[:, None, :]], axis=1)
        conv_act = jax.nn.silu(lax.optimization_barrier(jnp.sum(window * conv_weight[None], axis=1)) + conv_bias).astype(jnp.bfloat16)
        conv_state = window[:, 1:, :]
        projected = jnp.dot(conv_act, x_proj.T, preferred_element_type=jnp.float32)
        step_size = jax.nn.softplus(jnp.dot(projected[:, :DTR], dt_proj.astype(jnp.float32), precision=lax.Precision.HIGHEST) + dt_bias)
        input_map = projected[:, DTR:DTR + NS]
        output_map = projected[:, DTR + NS:]
        act_float = conv_act.astype(jnp.float32)
        ssm_state = jnp.exp(step_size[:, None, :] * decay_rate[None]) * ssm_state + step_size[:, None, :] * input_map[:, :, None] * act_float[:, None, :]
        gated = ((lax.optimization_barrier(jnp.sum(ssm_state * output_map[:, :, None], axis=1)) + d_skip * act_float) * jax.nn.silu(z_part)).astype(jnp.bfloat16)
        residual = inputs + jnp.dot(gated, out_proj, preferred_element_type=jnp.float32)
        routed = normalize(residual, moe_gain).astype(jnp.bfloat16)
        mixture = jnp.zeros_like(residual)
        limit = N_DP * N_EXPERT * CAP
        for expert in range(EW):
            named = route_ids[step_index] == expert
            weight = lax.optimization_barrier(jnp.sum(jnp.where(named, route_weights[step_index], 0.0), axis=1))
            chosen = jnp.any(named, axis=1)
            picked = jnp.nonzero(chosen, size=limit, fill_value=0)[0]
            valid = jnp.arange(limit) < jnp.sum(chosen.astype(jnp.int32))
            rows_in = routed[picked]
            gate_val = jnp.dot(rows_in, w_gate[expert].T, preferred_element_type=jnp.float32)
            up_val = jnp.dot(rows_in, w_up[expert].T, preferred_element_type=jnp.float32)
            hidden = (jax.nn.silu(gate_val) * up_val).astype(jnp.bfloat16)
            expert_out = jnp.dot(hidden, w_down[expert], preferred_element_type=jnp.float32).astype(jnp.bfloat16)
            factor = jnp.where(valid, weight[picked], 0.0)
            mixture = mixture.at[picked].add(factor[:, None] * expert_out.astype(jnp.float32))
        outputs.append((residual + mixture).astype(jnp.bfloat16))
    return (jnp.stack(outputs), ssm_state, conv_state)
```

```python
import functools

import jax
import jax.numpy as jnp
from jax import lax
from jax.experimental import pallas as pl
from jax.experimental.pallas import tpu as pltpu
from jax.sharding import PartitionSpec as P

CAP = 2
EPS = 1e-05
MIB = 1 << 20
F32 = jnp.float32
BF16 = jnp.bfloat16
VMEM = pl.BlockSpec(memory_space=pltpu.VMEM)
SMEM = pl.BlockSpec(memory_space=pltpu.SMEM)


def silu(values):
    return values / (1.0 + jnp.exp(-values))


def softplus(values):
    return jnp.maximum(values, 0.0) + jnp.log1p(jnp.exp(-jnp.abs(values)))


def normalize(values, gain):
    return values * lax.rsqrt(jnp.mean(values * values, axis=-1, keepdims=True) + EPS) * gain


def held(array):
    return pltpu.with_memory_space_constraint(array, pltpu.VMEM)


def call(body, name, outs, specs, args, scratch=(), flops=0, moved=0, limit=8):
    return pl.pallas_call(
        body,
        name=name,
        out_shape=[jax.ShapeDtypeStruct(s, d) for s, d in outs],
        in_specs=specs,
        out_specs=[VMEM] * len(outs),
        scratch_shapes=list(scratch),
        cost_estimate=pl.CostEstimate(flops=flops, bytes_accessed=moved, transcendentals=0),
        compiler_params=pltpu.CompilerParams(vmem_limit_bytes=limit * MIB),
    )(*args)


def levels_of(count):
    levels, stride = [], 1
    while count // stride > 2:
        size = 4 if count // stride >= 8 else 2
        levels.append((stride, size))
        stride *= size
    return levels, stride


def partner(array, distance, count):
    return lax.ppermute(array, "expert", [(i, i ^ distance) for i in range(count)])


def other_core(array):
    return lax.ppermute(array, "dp", [(0, 1), (1, 0)])


def total(parts):
    result = parts[0].astype(F32)
    for part in parts[1:]:
        result = result + part.astype(F32)
    return result


def spread(block, levels, count):
    parts = [block]
    for position, (stride, size) in enumerate(reversed(levels)):
        whole = parts[0] if position == 0 else jnp.concatenate(parts, axis=0)
        parts = [whole] + [partner(whole, k * stride, count) for k in range(1, size)]
    return parts


def collect(parts, levels, count):
    for position, (stride, size) in enumerate(levels):
        if position > 0:
            parts = jnp.split(parts, size, axis=0)
        parts = total([parts[0]] + [partner(parts[k], k * stride, count) for k in range(1, size)])
        parts = parts.astype(BF16)
    return parts[0] if isinstance(parts, list) else parts


def add_everywhere(parts, levels, count):
    for position, (stride, size) in enumerate(levels):
        if position > 0:
            rows, columns = parts.shape
            split = parts.reshape(stride, size, rows // (stride * size), columns)
            parts = [
                jnp.stack([split[:, j ^ k] for j in range(size)], axis=1).reshape(rows, columns)
                for k in range(size)
            ]
        sent = [partner(parts[k], k * stride, count) for k in range(1, size)]
        parts = total([parts[0]] + sent).astype(BF16)
    return parts[0] if isinstance(parts, list) else parts


def joined(refs):
    if len(refs) == 1:
        return refs[0][...]
    return jnp.concatenate([r[...].astype(F32) for r in refs], axis=0).astype(BF16)


def place_rows(scratch, own, peer, upper):
    rows = own.shape[0]

    @pl.when(upper == 0)
    def _():
        scratch[0:rows, :] = own
        scratch[rows : 2 * rows, :] = peer

    @pl.when(upper != 0)
    def _():
        scratch[0:rows, :] = peer
        scratch[rows : 2 * rows, :] = own


def start_body(where, own, peer, gain, x_out, normed_out):
    place_rows(x_out, own[0].astype(F32), peer[0].astype(F32), where[1])
    normed_out[...] = normalize(x_out[...], gain[...]).astype(BF16)


def table_body(steps, rows, where, own, peer, select_out, combine_out):
    slots = 4 * CAP
    span = 2 * rows
    slot_a = lax.broadcasted_iota(jnp.int32, (slots, span), 0)
    row_a = lax.broadcasted_iota(jnp.int32, (slots, span), 1)
    row_b = lax.broadcasted_iota(jnp.int32, (span, slots), 0)
    slot_b = lax.broadcasted_iota(jnp.int32, (span, slots), 1)
    for step in range(steps):
        select = jnp.zeros((slots, span), F32)
        combine = jnp.zeros((span, slots), F32)
        for far in range(2):
            expert = (where[2] if far == 0 else 1 - where[2]).astype(F32)
            for block in range(2):
                count = jnp.int32(0)
                for j in range(rows):
                    at = (step * rows + j) * 4
                    entry = [
                        jnp.where(where[1] == block, own[at + m], peer[at + m]) for m in range(4)
                    ]
                    first = entry[0] == expert
                    second = entry[1] == expert
                    weight = jnp.where(first, entry[2], 0.0) + jnp.where(second, entry[3], 0.0)
                    named = jnp.where(first | second, 1, 0)
                    row = block * rows + j
                    slot = jnp.where(named == 1, (far * 2 + block) * CAP + count, -1)
                    select = jnp.where((slot_a == slot) & (row_a == row), 1.0, select)
                    combine = jnp.where((slot_b == slot) & (row_b == row), weight, combine)
                    count = count + named
        select_out[step] = select
        combine_out[step] = combine


def row_of(index, rows, levels, stride, me):
    within = index % rows
    half = (index // rows) % 2
    rest = index // (2 * rows)
    distance = 0
    for level_stride, size in reversed(levels):
        distance += (rest % size) * level_stride
        rest //= size
    return (((me ^ distance) & (stride - 1)) + half * stride) * rows + within


def first_taps_body(rows, levels, stride, where, prompts, conv, *taps):
    for index in range(taps[0].shape[0]):
        prompt = prompts[row_of(index, rows, levels, stride, where[0])]
        for j, tap in enumerate(taps):
            tap[index : index + 1, :] = conv[prompt, j : j + 1, :]


def x_body(parts, taps, *refs):
    rows_in, refs = refs[:parts], refs[parts:]
    held_taps, refs = refs[:taps], refs[taps:]
    in_proj, conv_weight, conv_bias, x_proj, x_out, act_out, *proj_outs = refs
    x_part = jnp.dot(joined(rows_in), in_proj[0], preferred_element_type=F32)
    x_out[...] = x_part
    mixed = x_part * conv_weight[taps : taps + 1, :]
    for j in range(taps):
        mixed = mixed + held_taps[j][...] * conv_weight[j : j + 1, :]
    act = silu(mixed + conv_bias[...]).astype(BF16)
    act_out[...] = act
    proj = lax.dot_general(
        act, x_proj[...], (((1,), (1,)), ((), ())), preferred_element_type=F32
    )
    size = proj.shape[0] // parts
    pieces = [proj[k * size : (k + 1) * size] for k in range(parts)]
    for k, out in enumerate(proj_outs):
        out[...] = jnp.concatenate([pieces[j ^ k] for j in range(parts)], axis=0).astype(BF16)


def z_body(parts, *refs):
    rows_in, (in_proj, z_out) = refs[:parts], refs[parts:]
    z_out[...] = silu(jnp.dot(joined(rows_in), in_proj[1], preferred_element_type=F32))


def taps_out_body(rows, levels, stride, where, *refs):
    *taps, out = refs
    for index in range(taps[0].shape[0]):
        row = row_of(index, rows, levels, stride, where[0])
        for j, tap in enumerate(taps):
            out[row, j : j + 1, :] = tap[index : index + 1, :]


def ssm_body(first, parts, rows, levels, stride, *refs):
    where, prompts, near, far, act_in, z_in, dt_proj, dt_bias, a_log, d_skip, out_proj, before = (
        refs[:12]
    )
    outs, (after, y) = refs[12 : 12 + parts], refs[12 + parts :]
    rank = dt_proj.shape[0]
    states = a_log.shape[0]
    projected = near[...].astype(F32) + far[...].astype(F32)
    step_in = projected[:, :rank]
    high = step_in.astype(BF16)
    low = (step_in - high.astype(F32)).astype(BF16)
    delta = softplus(
        jnp.dot(high, dt_proj[...], preferred_element_type=F32)
        + jnp.dot(low, dt_proj[...], preferred_element_type=F32)
        + dt_bias[...]
    )
    maps = jnp.transpose(projected[:, rank:])
    act = act_in[...].astype(F32)
    driven = delta * act
    decay = -jnp.exp(a_log[...])
    for index in range(delta.shape[0]):
        row = row_of(index, rows, levels, stride, where[0])
        held_state = before[prompts[row]] if first else before[row]
        state = (
            jnp.exp(delta[index : index + 1, :] * decay) * held_state
            + driven[index : index + 1, :] * maps[:states, index : index + 1]
        )
        after[row] = state
        y[index : index + 1, :] = jnp.sum(
            state * maps[states:, index : index + 1], axis=0, keepdims=True
        )
    gated = ((y[...] + d_skip[...] * act) * z_in[...]).astype(BF16)
    mixed = jnp.dot(gated, out_proj[...], preferred_element_type=F32)
    size = mixed.shape[0] // parts
    for k, out in enumerate(outs):
        out[...] = mixed[k * size : (k + 1) * size].astype(BF16)


def route_body(near, far, x_in, gain, select, h_out, own_out, other_out):
    h = x_in[...] + (near[...].astype(F32) + far[...].astype(F32))
    h_out[...] = h
    routed = normalize(h, gain[...])
    picked = select[:, 0:1] * routed[0:1, :]
    for r in range(1, h.shape[0]):
        picked = picked + select[:, r : r + 1] * routed[r : r + 1, :]
    half = picked.shape[0] // 2
    own_out[...] = picked[:half].astype(BF16)
    other_out[...] = picked[half:].astype(BF16)


def expert_body(parts, *refs):
    rows_in, (gate, up, down) = refs[:parts], refs[parts : parts + 3]
    outs = refs[parts + 3 :]
    rows = joined(rows_in)
    dims = (((1,), (1,)), ((), ()))
    gate_val = lax.dot_general(rows, gate[...], dims, preferred_element_type=F32)
    up_val = lax.dot_general(rows, up[...], dims, preferred_element_type=F32)
    hidden = (silu(gate_val) * up_val).astype(BF16)
    result = jnp.dot(hidden, down[...], preferred_element_type=F32)
    size = result.shape[0] // parts
    for k, out in enumerate(outs):
        out[...] = result[k * size : (k + 1) * size].astype(BF16)


def combined(h_in, near, far, combine):
    half = far.shape[0]
    result = h_in[...]
    near_rows = near[...].astype(F32)
    far_rows = far[...].astype(F32)
    mixture = combine[:, 0:1] * near_rows[0:1, :]
    for s in range(1, half):
        mixture = mixture + combine[:, s : s + 1] * near_rows[s : s + 1, :]
    for s in range(half):
        mixture = mixture + combine[:, half + s : half + s + 1] * far_rows[s : s + 1, :]
    return (result + mixture).astype(BF16).astype(F32)


def store_own(out, rows, values, upper):
    @pl.when(upper == 0)
    def _():
        out[...] = values[:rows].astype(BF16)

    @pl.when(upper != 0)
    def _():
        out[...] = values[rows:].astype(BF16)


def next_body(step, where, h_in, near, far, combine, own, peer, gain, out, x_out, normed_out):
    values = combined(h_in, near, far, combine)
    store_own(out, out.shape[0], values, where[1])
    place_rows(x_out, own[step + 1].astype(F32), peer[step + 1].astype(F32), where[1])
    x = values + x_out[...]
    x_out[...] = x
    normed_out[...] = normalize(x, gain[...]).astype(BF16)


def last_body(earlier, where, h_in, near, far, combine, *refs):
    before, out = refs[:earlier], refs[earlier]
    values = combined(h_in, near, far, combine)
    for step in range(earlier):
        out[step] = before[step][...]
    store_own(out.at[earlier], out.shape[1], values, where[1])


def on_device(
    layer_input,
    prompt_ssm,
    prompt_conv,
    sample_prompt,
    mamba_gain,
    in_proj,
    conv_weight,
    conv_bias,
    x_proj,
    dt_proj,
    dt_bias,
    a_log,
    d_skip,
    out_proj,
    moe_gain,
    route_ids,
    route_weights,
    w_gate,
    w_up,
    w_down,
):
    count = lax.axis_size("expert")
    levels, stride = levels_of(count)
    parts = levels[0][1] if levels else 1
    steps, rows, width = layer_input.shape
    group_rows = rows * count
    channels = in_proj.shape[2]
    taps = prompt_conv.shape[1]
    states = a_log.shape[0]
    slots = 2 * 2 * CAP
    me = lax.axis_index("expert")
    core = lax.axis_index("dp")
    where = jnp.stack([me, me // stride, core]).astype(jnp.int32)

    peer_input = partner(layer_input, stride, count)
    routes = jnp.concatenate([route_ids.astype(F32), route_weights], axis=2)
    peer_routes = partner(routes, stride, count)
    peer_ssm = other_core(prompt_ssm)
    peer_conv = other_core(prompt_conv)
    all_ssm = jnp.where(
        core == 0,
        jnp.concatenate([prompt_ssm, peer_ssm]),
        jnp.concatenate([peer_ssm, prompt_ssm]),
    )
    all_conv = jnp.where(
        core == 0,
        jnp.concatenate([prompt_conv, peer_conv]),
        jnp.concatenate([peer_conv, prompt_conv]),
    )
    mamba_gain = mamba_gain.reshape(1, width)
    moe_gain = moe_gain.reshape(1, width)
    conv_bias = conv_bias.reshape(1, channels)
    dt_bias = dt_bias.reshape(1, channels)
    d_skip = d_skip.reshape(1, channels)
    gate, up, down = w_gate[0], w_up[0], w_down[0]
    place = (rows, levels, stride)

    x, normed = call(
        start_body,
        "first_norm",
        [((2 * rows, width), F32), ((2 * rows, width), BF16)],
        [SMEM, VMEM, VMEM, VMEM],
        (where, layer_input, peer_input, mamba_gain),
    )
    select, combine = call(
        functools.partial(table_body, steps, rows),
        "route_tables",
        [((steps, slots, 2 * rows), F32), ((steps, 2 * rows, slots), F32)],
        [SMEM, SMEM, SMEM],
        (where, routes.reshape(-1), peer_routes.reshape(-1)),
    )
    window = call(
        functools.partial(first_taps_body, *place),
        "first_taps",
        [((group_rows, channels), F32)] * taps,
        [SMEM, SMEM, VMEM],
        (where, sample_prompt, all_conv),
    )
    state = all_ssm
    outputs = []
    for step in range(steps):
        last = step == steps - 1
        rows_in = spread(normed, levels, count)
        x_part, act, *proj = call(
            functools.partial(x_body, parts, taps),
            "mamba_x",
            [
                ((group_rows, channels), F32),
                ((group_rows, channels), BF16),
            ]
            + [((group_rows, x_proj.shape[0]), BF16)] * parts,
            [VMEM] * (parts + taps + 4),
            (*rows_in, *window, held(in_proj), conv_weight, conv_bias, held(x_proj)),
            flops=2 * group_rows * width * channels,
            moved=2 * width * channels,
        )
        window = [*window[1:], x_part]
        proj = add_everywhere(proj, levels, count)
        proj_far = partner(proj, stride, count)
        z_gate = call(
            functools.partial(z_body, parts),
            "mamba_z",
            [((group_rows, channels), F32)],
            [VMEM] * (parts + 1),
            (*rows_in, held(in_proj)),
            flops=2 * group_rows * width * channels,
            moved=2 * width * channels,
        )[0]
        if last:
            conv_state = call(
                functools.partial(taps_out_body, *place),
                "taps_out",
                [((group_rows, taps, channels), F32)],
                [SMEM] + [VMEM] * taps,
                (where, *window),
            )[0]
        *mixed, state = call(
            functools.partial(ssm_body, step == 0, parts, *place),
            "mamba_ssm",
            [((group_rows // parts, width), BF16)] * parts
            + [((group_rows, states, channels), F32)],
            [SMEM, SMEM] + [VMEM] * 10,
            (
                where,
                sample_prompt,
                proj,
                proj_far,
                act,
                z_gate,
                held(dt_proj),
                dt_bias,
                a_log,
                d_skip,
                held(out_proj),
                state,
            ),
            scratch=[pltpu.VMEM((group_rows, channels), F32)],
            flops=2 * group_rows * width * channels,
            moved=2 * width * channels,
        )
        mixed_near = collect(mixed, levels, count)
        mixed_far = partner(mixed_near, stride, count)
        h, own, other = call(
            route_body,
            "route",
            [
                ((2 * rows, width), F32),
                ((slots // 2, width), BF16),
                ((slots // 2, width), BF16),
            ],
            [VMEM] * 5,
            (mixed_near, mixed_far, x, moe_gain, select[step]),
        )
        picked = spread(jnp.concatenate([own, other_core(other)]), levels, count)
        total_slots = slots * (count // 2)
        returned = call(
            functools.partial(expert_body, parts),
            "experts",
            [((total_slots // parts, width), BF16)] * parts,
            [VMEM] * (parts + 3),
            (*picked, held(gate), held(up), held(down)),
            flops=6 * total_slots * width * gate.shape[0],
            moved=6 * width * gate.shape[0],
        )
        out_near = collect(returned, levels, count)
        summed = total([out_near, partner(out_near, stride, count)]).astype(BF16)
        out_far = other_core(summed[slots // 2 :])
        if last:
            layer_output = call(
                functools.partial(last_body, step),
                "last_output",
                [((steps, rows, width), BF16)],
                [SMEM] + [VMEM] * (4 + step),
                (where, h, summed, out_far, combine[step], *outputs),
            )[0]
        else:
            out, x, normed = call(
                functools.partial(next_body, step),
                "next_norm",
                [
                    ((rows, width), BF16),
                    ((2 * rows, width), F32),
                    ((2 * rows, width), BF16),
                ],
                [SMEM] + [VMEM] * 7,
                (where, h, summed, out_far, combine[step], layer_input, peer_input, mamba_gain),
            )
            outputs.append(out)
    return (layer_output, state, conv_state)


def solution(mesh):
    in_specs = (
        P(None, ("group", "dp", "expert"), None),
        P(("group", "dp"), None, "expert"),
        P(("group", "dp"), None, "expert"),
        P(("group", "dp")),
        P(),
        P(None, None, "expert"),
        P(None, "expert"),
        P("expert"),
        P(None, "expert"),
        P(None, "expert"),
        P("expert"),
        P(None, "expert"),
        P("expert"),
        P("expert", None),
        P(),
        P(None, ("group", "dp", "expert"), None),
        P(None, ("group", "dp", "expert"), None),
        P("dp", "expert", None),
        P("dp", "expert", None),
        P("dp", "expert", None),
    )
    out_specs = (
        P(None, ("group", "dp", "expert"), None),
        P(("group", "dp"), None, "expert"),
        P(("group", "dp"), None, "expert"),
    )
    return jax.shard_map(
        on_device, mesh=mesh, in_specs=in_specs, out_specs=out_specs, check_vma=False
    )
```

```python
import functools

import jax
import jax.numpy as jnp
from jax import lax
from jax.experimental import pallas as pl
from jax.experimental.pallas import tpu as pltpu
from jax.sharding import PartitionSpec as P

CAP = 2
EPS = 1e-05
MIB = 1 << 20
BESIDE = 10**10
F32 = jnp.float32
BF16 = jnp.bfloat16
VMEM = pl.BlockSpec(memory_space=pltpu.VMEM)
SMEM = pl.BlockSpec(memory_space=pltpu.SMEM)


def silu(values):
    return values / (1.0 + jnp.exp(-values))


def softplus(values):
    return jnp.maximum(values, 0.0) + jnp.log1p(jnp.exp(-jnp.abs(values)))


def normalize(values, gain):
    return values * lax.rsqrt(jnp.mean(values * values, axis=-1, keepdims=True) + EPS) * gain


def held(array):
    return pltpu.with_memory_space_constraint(array, pltpu.VMEM)


def call(body, name, outs, specs, args, scratch=(), flops=0, moved=0, limit=8):
    flops = max(flops, BESIDE)
    return pl.pallas_call(
        body,
        name=name,
        out_shape=[jax.ShapeDtypeStruct(s, d) for s, d in outs],
        in_specs=specs,
        out_specs=[VMEM] * len(outs),
        scratch_shapes=list(scratch),
        cost_estimate=pl.CostEstimate(flops=flops, bytes_accessed=moved, transcendentals=0),
        compiler_params=pltpu.CompilerParams(vmem_limit_bytes=limit * MIB),
    )(*args)


def levels_of(count):
    levels, stride = [], 1
    while count // stride > 2:
        size = 4 if count // stride >= 8 else 2
        levels.append((stride, size))
        stride *= size
    return levels, stride


def partner(array, distance, count):
    return lax.ppermute(array, "expert", [(i, i ^ distance) for i in range(count)])


def other_core(array):
    return lax.ppermute(array, "dp", [(0, 1), (1, 0)])


def total(parts):
    result = parts[0].astype(F32)
    for part in parts[1:]:
        result = result + part.astype(F32)
    return result


def spread(block, levels, count):
    parts = [block]
    for position, (stride, size) in enumerate(reversed(levels)):
        whole = parts[0] if position == 0 else jnp.concatenate(parts, axis=0)
        parts = [whole] + [partner(whole, k * stride, count) for k in range(1, size)]
    return parts


def collect(parts, levels, count):
    for position, (stride, size) in enumerate(levels):
        if position > 0:
            parts = jnp.split(parts, size, axis=0)
        parts = total([parts[0]] + [partner(parts[k], k * stride, count) for k in range(1, size)])
        parts = parts.astype(BF16)
    return parts[0] if isinstance(parts, list) else parts


def add_everywhere(parts, levels, count):
    for position, (stride, size) in enumerate(levels):
        if position > 0:
            rows, columns = parts.shape
            split = parts.reshape(stride, size, rows // (stride * size), columns)
            parts = [
                jnp.stack([split[:, j ^ k] for j in range(size)], axis=1).reshape(rows, columns)
                for k in range(size)
            ]
        sent = [partner(parts[k], k * stride, count) for k in range(1, size)]
        parts = total([parts[0]] + sent).astype(BF16)
    return parts[0] if isinstance(parts, list) else parts


def joined(refs):
    if len(refs) == 1:
        return refs[0][...]
    return jnp.concatenate([r[...].astype(F32) for r in refs], axis=0).astype(BF16)


def place_rows(scratch, own, peer, upper):
    rows = own.shape[0]

    @pl.when(upper == 0)
    def _():
        scratch[0:rows, :] = own
        scratch[rows : 2 * rows, :] = peer

    @pl.when(upper != 0)
    def _():
        scratch[0:rows, :] = peer
        scratch[rows : 2 * rows, :] = own


def start_body(where, own, peer, gain, x_out, normed_out):
    place_rows(x_out, own[0].astype(F32), peer[0].astype(F32), where[1])
    normed_out[...] = normalize(x_out[...], gain[...]).astype(BF16)


def table_body(steps, rows, where, own, peer, select_out, combine_out):
    slots = 4 * CAP
    span = 2 * rows
    slot_a = lax.broadcasted_iota(jnp.int32, (slots, span), 0)
    row_a = lax.broadcasted_iota(jnp.int32, (slots, span), 1)
    row_b = lax.broadcasted_iota(jnp.int32, (span, slots), 0)
    slot_b = lax.broadcasted_iota(jnp.int32, (span, slots), 1)
    for step in range(steps):
        select = jnp.zeros((slots, span), F32)
        combine = jnp.zeros((span, slots), F32)
        for far in range(2):
            expert = (where[2] if far == 0 else 1 - where[2]).astype(F32)
            for block in range(2):
                count = jnp.int32(0)
                for j in range(rows):
                    at = (step * rows + j) * 4
                    entry = [
                        jnp.where(where[1] == block, own[at + m], peer[at + m]) for m in range(4)
                    ]
                    first = entry[0] == expert
                    second = entry[1] == expert
                    weight = jnp.where(first, entry[2], 0.0) + jnp.where(second, entry[3], 0.0)
                    named = jnp.where(first | second, 1, 0)
                    row = block * rows + j
                    slot = jnp.where(named == 1, (far * 2 + block) * CAP + count, -1)
                    select = jnp.where((slot_a == slot) & (row_a == row), 1.0, select)
                    combine = jnp.where((slot_b == slot) & (row_b == row), weight, combine)
                    count = count + named
        select_out[step] = select
        combine_out[step] = combine


def row_of(index, rows, levels, stride, me):
    within = index % rows
    half = (index // rows) % 2
    rest = index // (2 * rows)
    distance = 0
    for level_stride, size in reversed(levels):
        distance += (rest % size) * level_stride
        rest //= size
    return (((me ^ distance) & (stride - 1)) + half * stride) * rows + within


def first_taps_body(rows, levels, stride, where, prompts, conv, *taps):
    for index in range(taps[0].shape[0]):
        prompt = prompts[row_of(index, rows, levels, stride, where[0])]
        for j, tap in enumerate(taps):
            tap[index : index + 1, :] = conv[prompt, j : j + 1, :]


def x_body(parts, taps, *refs):
    rows_in, refs = refs[:parts], refs[parts:]
    held_taps, refs = refs[:taps], refs[taps:]
    in_proj, conv_weight, conv_bias, x_proj, x_out, act_out, *proj_outs = refs
    x_part = jnp.dot(joined(rows_in), in_proj[0], preferred_element_type=F32)
    x_out[...] = x_part
    mixed = x_part * conv_weight[taps : taps + 1, :]
    for j in range(taps):
        mixed = mixed + held_taps[j][...] * conv_weight[j : j + 1, :]
    act = silu(mixed + conv_bias[...]).astype(BF16)
    act_out[...] = act
    proj = lax.dot_general(
        act, x_proj[...], (((1,), (1,)), ((), ())), preferred_element_type=F32
    )
    size = proj.shape[0] // parts
    pieces = [proj[k * size : (k + 1) * size] for k in range(parts)]
    for k, out in enumerate(proj_outs):
        out[...] = jnp.concatenate([pieces[j ^ k] for j in range(parts)], axis=0).astype(BF16)


def z_body(parts, *refs):
    rows_in, (in_proj, z_out) = refs[:parts], refs[parts:]
    z_out[...] = silu(jnp.dot(joined(rows_in), in_proj[1], preferred_element_type=F32))


def taps_out_body(rows, levels, stride, where, *refs):
    *taps, out = refs
    for index in range(taps[0].shape[0]):
        row = row_of(index, rows, levels, stride, where[0])
        for j, tap in enumerate(taps):
            out[row, j : j + 1, :] = tap[index : index + 1, :]


def ssm_body(first, parts, rows, levels, stride, *refs):
    where, prompts, near, far, act_in, z_in, dt_proj, dt_bias, a_log, d_skip, out_proj, before = (
        refs[:12]
    )
    outs, (after, y) = refs[12 : 12 + parts], refs[12 + parts :]
    rank = dt_proj.shape[0]
    states = a_log.shape[0]
    projected = near[...].astype(F32) + far[...].astype(F32)
    step_in = projected[:, :rank]
    high = step_in.astype(BF16)
    low = (step_in - high.astype(F32)).astype(BF16)
    delta = softplus(
        jnp.dot(high, dt_proj[...], preferred_element_type=F32)
        + jnp.dot(low, dt_proj[...], preferred_element_type=F32)
        + dt_bias[...]
    )
    maps = jnp.transpose(projected[:, rank:])
    act = act_in[...].astype(F32)
    driven = delta * act
    decay = -jnp.exp(a_log[...])
    for index in range(delta.shape[0]):
        row = row_of(index, rows, levels, stride, where[0])
        held_state = before[prompts[row]] if first else before[row]
        state = (
            jnp.exp(delta[index : index + 1, :] * decay) * held_state
            + driven[index : index + 1, :] * maps[:states, index : index + 1]
        )
        after[row] = state
        y[index : index + 1, :] = jnp.sum(
            state * maps[states:, index : index + 1], axis=0, keepdims=True
        )
    gated = ((y[...] + d_skip[...] * act) * z_in[...]).astype(BF16)
    mixed = jnp.dot(gated, out_proj[...], preferred_element_type=F32)
    size = mixed.shape[0] // parts
    for k, out in enumerate(outs):
        out[...] = mixed[k * size : (k + 1) * size].astype(BF16)


def route_body(near, far, x_in, gain, select, h_out, own_out, other_out):
    h = x_in[...] + (near[...].astype(F32) + far[...].astype(F32))
    h_out[...] = h
    routed = normalize(h, gain[...])
    picked = select[:, 0:1] * routed[0:1, :]
    for r in range(1, h.shape[0]):
        picked = picked + select[:, r : r + 1] * routed[r : r + 1, :]
    half = picked.shape[0] // 2
    own_out[...] = picked[:half].astype(BF16)
    other_out[...] = picked[half:].astype(BF16)


def expert_body(parts, *refs):
    rows_in, (gate, up, down) = refs[:parts], refs[parts : parts + 3]
    outs = refs[parts + 3 :]
    rows = joined(rows_in)
    dims = (((1,), (1,)), ((), ()))
    gate_val = lax.dot_general(rows, gate[...], dims, preferred_element_type=F32)
    up_val = lax.dot_general(rows, up[...], dims, preferred_element_type=F32)
    hidden = (silu(gate_val) * up_val).astype(BF16)
    result = jnp.dot(hidden, down[...], preferred_element_type=F32)
    size = result.shape[0] // parts
    for k, out in enumerate(outs):
        out[...] = result[k * size : (k + 1) * size].astype(BF16)


def combined(h_in, near, far, combine):
    half = far.shape[0]
    result = h_in[...]
    near_rows = near[...].astype(F32)
    far_rows = far[...].astype(F32)
    mixture = combine[:, 0:1] * near_rows[0:1, :]
    for s in range(1, half):
        mixture = mixture + combine[:, s : s + 1] * near_rows[s : s + 1, :]
    for s in range(half):
        mixture = mixture + combine[:, half + s : half + s + 1] * far_rows[s : s + 1, :]
    return (result + mixture).astype(BF16).astype(F32)


def store_own(out, rows, values, upper):
    @pl.when(upper == 0)
    def _():
        out[...] = values[:rows].astype(BF16)

    @pl.when(upper != 0)
    def _():
        out[...] = values[rows:].astype(BF16)


def next_body(step, where, h_in, near, far, combine, own, peer, gain, out, x_out, normed_out):
    values = combined(h_in, near, far, combine)
    store_own(out, out.shape[0], values, where[1])
    place_rows(x_out, own[step + 1].astype(F32), peer[step + 1].astype(F32), where[1])
    x = values + x_out[...]
    x_out[...] = x
    normed_out[...] = normalize(x, gain[...]).astype(BF16)


def last_body(earlier, where, h_in, near, far, combine, *refs):
    before, out = refs[:earlier], refs[earlier]
    values = combined(h_in, near, far, combine)
    for step in range(earlier):
        out[step] = before[step][...]
    store_own(out.at[earlier], out.shape[1], values, where[1])


def on_device(
    layer_input,
    prompt_ssm,
    prompt_conv,
    sample_prompt,
    mamba_gain,
    in_proj,
    conv_weight,
    conv_bias,
    x_proj,
    dt_proj,
    dt_bias,
    a_log,
    d_skip,
    out_proj,
    moe_gain,
    route_ids,
    route_weights,
    w_gate,
    w_up,
    w_down,
):
    count = lax.axis_size("expert")
    levels, stride = levels_of(count)
    parts = levels[0][1] if levels else 1
    steps, rows, width = layer_input.shape
    group_rows = rows * count
    channels = in_proj.shape[2]
    taps = prompt_conv.shape[1]
    states = a_log.shape[0]
    slots = 2 * 2 * CAP
    me = lax.axis_index("expert")
    core = lax.axis_index("dp")
    where = jnp.stack([me, me // stride, core]).astype(jnp.int32)

    peer_input = partner(layer_input, stride, count)
    routes = jnp.concatenate([route_ids.astype(F32), route_weights], axis=2)
    peer_routes = partner(routes, stride, count)
    peer_ssm = other_core(prompt_ssm)
    peer_conv = other_core(prompt_conv)
    all_ssm = jnp.where(
        core == 0,
        jnp.concatenate([prompt_ssm, peer_ssm]),
        jnp.concatenate([peer_ssm, prompt_ssm]),
    )
    all_conv = jnp.where(
        core == 0,
        jnp.concatenate([prompt_conv, peer_conv]),
        jnp.concatenate([peer_conv, prompt_conv]),
    )
    mamba_gain = mamba_gain.reshape(1, width)
    moe_gain = moe_gain.reshape(1, width)
    conv_bias = conv_bias.reshape(1, channels)
    dt_bias = dt_bias.reshape(1, channels)
    d_skip = d_skip.reshape(1, channels)
    gate, up, down = w_gate[0], w_up[0], w_down[0]
    place = (rows, levels, stride)

    x, normed = call(
        start_body,
        "first_norm",
        [((2 * rows, width), F32), ((2 * rows, width), BF16)],
        [SMEM, VMEM, VMEM, VMEM],
        (where, layer_input, peer_input, mamba_gain),
    )
    select, combine = call(
        functools.partial(table_body, steps, rows),
        "route_tables",
        [((steps, slots, 2 * rows), F32), ((steps, 2 * rows, slots), F32)],
        [SMEM, SMEM, SMEM],
        (where, routes.reshape(-1), peer_routes.reshape(-1)),
    )
    window = call(
        functools.partial(first_taps_body, *place),
        "first_taps",
        [((group_rows, channels), F32)] * taps,
        [SMEM, SMEM, VMEM],
        (where, sample_prompt, all_conv),
    )
    state = all_ssm
    outputs = []
    for step in range(steps):
        last = step == steps - 1
        rows_in = spread(normed, levels, count)
        if step == 0:
            rows_in, select, combine, window, state = lax.optimization_barrier(
                (rows_in, select, combine, window, state)
            )
        x_part, act, *proj = call(
            functools.partial(x_body, parts, taps),
            "mamba_x",
            [
                ((group_rows, channels), F32),
                ((group_rows, channels), BF16),
            ]
            + [((group_rows, x_proj.shape[0]), BF16)] * parts,
            [VMEM] * (parts + taps + 4),
            (*rows_in, *window, held(in_proj), conv_weight, conv_bias, held(x_proj)),
            flops=2 * group_rows * width * channels,
            moved=2 * width * channels,
        )
        window = [*window[1:], x_part]
        proj = add_everywhere(proj, levels, count)
        proj_far = partner(proj, stride, count)
        z_gate = call(
            functools.partial(z_body, parts),
            "mamba_z",
            [((group_rows, channels), F32)],
            [VMEM] * (parts + 1),
            (*rows_in, held(in_proj)),
            flops=2 * group_rows * width * channels,
            moved=2 * width * channels,
        )[0]
        if last:
            conv_state = call(
                functools.partial(taps_out_body, *place),
                "taps_out",
                [((group_rows, taps, channels), F32)],
                [SMEM] + [VMEM] * taps,
                (where, *window),
            )[0]
            proj_far, conv_state = lax.optimization_barrier((proj_far, conv_state))
        *mixed, state = call(
            functools.partial(ssm_body, step == 0, parts, *place),
            "mamba_ssm",
            [((group_rows // parts, width), BF16)] * parts
            + [((group_rows, states, channels), F32)],
            [SMEM, SMEM] + [VMEM] * 10,
            (
                where,
                sample_prompt,
                proj,
                proj_far,
                act,
                z_gate,
                held(dt_proj),
                dt_bias,
                a_log,
                d_skip,
                held(out_proj),
                state,
            ),
            scratch=[pltpu.VMEM((group_rows, channels), F32)],
            flops=2 * group_rows * width * channels,
            moved=2 * width * channels,
        )
        mixed_near = collect(mixed, levels, count)
        mixed_far = partner(mixed_near, stride, count)
        h, own, other = call(
            route_body,
            "route",
            [
                ((2 * rows, width), F32),
                ((slots // 2, width), BF16),
                ((slots // 2, width), BF16),
            ],
            [VMEM] * 5,
            (mixed_near, mixed_far, x, moe_gain, select[step]),
        )
        picked = spread(jnp.concatenate([own, other_core(other)]), levels, count)
        total_slots = slots * (count // 2)
        returned = call(
            functools.partial(expert_body, parts),
            "experts",
            [((total_slots // parts, width), BF16)] * parts,
            [VMEM] * (parts + 3),
            (*picked, held(gate), held(up), held(down)),
            flops=6 * total_slots * width * gate.shape[0],
            moved=6 * width * gate.shape[0],
        )
        out_near = collect(returned, levels, count)
        summed = total([out_near, partner(out_near, stride, count)]).astype(BF16)
        out_far = other_core(summed[slots // 2 :])
        if last:
            layer_output = call(
                functools.partial(last_body, step),
                "last_output",
                [((steps, rows, width), BF16)],
                [SMEM] + [VMEM] * (4 + step),
                (where, h, summed, out_far, combine[step], *outputs),
            )[0]
        else:
            out, x, normed = call(
                functools.partial(next_body, step),
                "next_norm",
                [
                    ((rows, width), BF16),
                    ((2 * rows, width), F32),
                    ((2 * rows, width), BF16),
                ],
                [SMEM] + [VMEM] * 7,
                (where, h, summed, out_far, combine[step], layer_input, peer_input, mamba_gain),
            )
            outputs.append(out)
    return (layer_output, state, conv_state)


def solution(mesh):
    in_specs = (
        P(None, ("group", "dp", "expert"), None),
        P(("group", "dp"), None, "expert"),
        P(("group", "dp"), None, "expert"),
        P(("group", "dp")),
        P(),
        P(None, None, "expert"),
        P(None, "expert"),
        P("expert"),
        P(None, "expert"),
        P(None, "expert"),
        P("expert"),
        P(None, "expert"),
        P("expert"),
        P("expert", None),
        P(),
        P(None, ("group", "dp", "expert"), None),
        P(None, ("group", "dp", "expert"), None),
        P("dp", "expert", None),
        P("dp", "expert", None),
        P("dp", "expert", None),
    )
    out_specs = (
        P(None, ("group", "dp", "expert"), None),
        P(("group", "dp"), None, "expert"),
        P(("group", "dp"), None, "expert"),
    )
    return jax.shard_map(
        on_device, mesh=mesh, in_specs=in_specs, out_specs=out_specs, check_vma=False
    )
```

```python
import functools

import jax
import jax.numpy as jnp
from jax import lax
from jax.experimental import pallas as pl
from jax.experimental.pallas import tpu as pltpu
from jax.sharding import PartitionSpec as P

CAP = 2
EPS = 1e-05
MIB = 1 << 20
BESIDE = 10**10
F32 = jnp.float32
BF16 = jnp.bfloat16
VMEM = pl.BlockSpec(memory_space=pltpu.VMEM)
SMEM = pl.BlockSpec(memory_space=pltpu.SMEM)
ANY = pl.BlockSpec(memory_space=pl.ANY)


def silu(values):
    return values / (1.0 + jnp.exp(-values))


def softplus(values):
    return jnp.maximum(values, 0.0) + jnp.log1p(jnp.exp(-jnp.abs(values)))


def normalize(values, gain):
    return values * lax.rsqrt(jnp.mean(values * values, axis=-1, keepdims=True) + EPS) * gain


def held(array):
    return pltpu.with_memory_space_constraint(array, pltpu.VMEM)


def in_hbm(array):
    return pltpu.with_memory_space_constraint(array, pltpu.HBM)


def call(body, name, outs, specs, args, scratch=(), flops=0, moved=0, limit=8):
    flops = max(flops, BESIDE)
    return pl.pallas_call(
        body,
        name=name,
        out_shape=[jax.ShapeDtypeStruct(s, d) for s, d in outs],
        in_specs=specs,
        out_specs=[VMEM] * len(outs),
        scratch_shapes=list(scratch),
        cost_estimate=pl.CostEstimate(flops=flops, bytes_accessed=moved, transcendentals=0),
        compiler_params=pltpu.CompilerParams(vmem_limit_bytes=limit * MIB),
    )(*args)


def levels_of(count):
    levels, stride = [], 1
    while count // stride > 2:
        size = 4 if count // stride >= 8 else 2
        levels.append((stride, size))
        stride *= size
    return levels, stride


def partner(array, distance, count):
    return lax.ppermute(array, "expert", [(i, i ^ distance) for i in range(count)])


def other_core(array):
    return lax.ppermute(array, "dp", [(0, 1), (1, 0)])


def across(array, distance, count):
    pairs = [(i, count + (i ^ distance)) for i in range(count)]
    return lax.ppermute(array, ("dp", "expert"), pairs + [(b, a) for a, b in pairs])


def total(parts):
    result = parts[0].astype(F32)
    for part in parts[1:]:
        result = result + part.astype(F32)
    return result


def spread(block, levels, count):
    parts = [block]
    for position, (stride, size) in enumerate(reversed(levels)):
        whole = parts[0] if position == 0 else jnp.concatenate(parts, axis=0)
        parts = [whole] + [partner(whole, k * stride, count) for k in range(1, size)]
    return parts


def collect(parts, levels, count, beside=()):
    for position, (stride, size) in enumerate(levels):
        if position > 0:
            parts = jnp.split(parts, size, axis=0)
        parts = [parts[0]] + [partner(parts[k], k * stride, count) for k in range(1, size)]
        if position == 0 and beside:
            parts[1], beside = lax.optimization_barrier((parts[1], beside))
        parts = total(parts).astype(BF16)
    return parts, beside


def add_everywhere(parts, levels, count):
    for position, (stride, size) in enumerate(levels):
        if position == 0:
            parts = [across(parts[k], k * stride, count) for k in range(size)]
        else:
            rows, columns = parts.shape
            split = parts.reshape(stride, size, rows // (stride * size), columns)
            parts = [
                jnp.stack([split[:, j ^ k] for j in range(size)], axis=1).reshape(rows, columns)
                for k in range(size)
            ]
            parts = [parts[0]] + [partner(parts[k], k * stride, count) for k in range(1, size)]
        parts = total(parts).astype(BF16)
    return parts


def back_from_halves(array, stride, count):
    return across(array, 0, count), across(array, stride, count)


def joined(refs):
    if len(refs) == 1:
        return refs[0][...]
    return jnp.concatenate([r[...].astype(F32) for r in refs], axis=0).astype(BF16)


def place_rows(scratch, own, peer, upper):
    rows = own.shape[0]

    @pl.when(upper == 0)
    def _():
        scratch[0:rows, :] = own
        scratch[rows : 2 * rows, :] = peer

    @pl.when(upper != 0)
    def _():
        scratch[0:rows, :] = peer
        scratch[rows : 2 * rows, :] = own


def start_body(where, own, peer, gain, x_out, normed_out, own_here, gain_here, arrived):
    copies = [
        pltpu.make_async_copy(own, own_here, arrived.at[0]),
        pltpu.make_async_copy(gain, gain_here, arrived.at[1]),
    ]
    for copy in copies:
        copy.start()
    for copy in copies:
        copy.wait()
    place_rows(x_out, own_here[0].astype(F32), peer[0].astype(F32), where[1])
    normed_out[...] = normalize(x_out[...], gain_here[...]).astype(BF16)


def later_body(steps, where, own, peer, *outs):
    for step in range(1, steps):
        place_rows(outs[step - 1], own[step].astype(F32), peer[step].astype(F32), where[1])


def table_body(steps, rows, where, own, peer, select_out, combine_out):
    slots = 4 * CAP
    span = 2 * rows
    slot_a = lax.broadcasted_iota(jnp.int32, (slots, span), 0)
    row_a = lax.broadcasted_iota(jnp.int32, (slots, span), 1)
    row_b = lax.broadcasted_iota(jnp.int32, (span, slots), 0)
    slot_b = lax.broadcasted_iota(jnp.int32, (span, slots), 1)
    for step in range(steps):
        select = jnp.zeros((slots, span), F32)
        combine = jnp.zeros((span, slots), F32)
        for far in range(2):
            expert = (where[2] if far == 0 else 1 - where[2]).astype(F32)
            for block in range(2):
                count = jnp.int32(0)
                for j in range(rows):
                    at = (step * rows + j) * 6
                    entry = [
                        jnp.where(where[1] == block, own[at + m], peer[at + m]) for m in range(6)
                    ]
                    first = entry[0] == expert
                    second = entry[1] == expert
                    weight = jnp.where(first, entry[2] + entry[4], 0.0) + jnp.where(
                        second, entry[3] + entry[5], 0.0
                    )
                    named = jnp.where(first | second, 1, 0)
                    row = block * rows + j
                    slot = jnp.where(named == 1, (far * 2 + block) * CAP + count, -1)
                    select = jnp.where((slot_a == slot) & (row_a == row), 1.0, select)
                    combine = jnp.where((slot_b == slot) & (row_b == row), weight, combine)
                    count = count + named
        select_out[step] = select
        combine_out[step] = combine


def row_of(index, rows, levels, stride, me):
    within = index % rows
    half = (index // rows) % 2
    rest = index // (2 * rows)
    distance = 0
    for level_stride, size in reversed(levels):
        distance += (rest % size) * level_stride
        rest //= size
    return (((me ^ distance) & (stride - 1)) + half * stride) * rows + within


def first_taps_body(rows, levels, stride, where, prompts, conv, *taps):
    for index in range(taps[0].shape[0]):
        prompt = prompts[row_of(index, rows, levels, stride, where[0])]
        for j, tap in enumerate(taps):
            tap[index : index + 1, :] = conv[prompt, j : j + 1, :]


def x_body(parts, taps, *refs):
    rows_in, refs = refs[:parts], refs[parts:]
    held_taps, refs = refs[:taps], refs[taps:]
    in_proj, conv_weight, conv_bias, x_proj, x_out, act_out, *proj_outs = refs
    x_part = jnp.dot(joined(rows_in), in_proj[0], preferred_element_type=F32)
    x_out[...] = x_part
    mixed = x_part * conv_weight[taps : taps + 1, :]
    for j in range(taps):
        mixed = mixed + held_taps[j][...] * conv_weight[j : j + 1, :]
    act = silu(mixed + conv_bias[...]).astype(BF16)
    act_out[...] = act
    proj = lax.dot_general(
        act, x_proj[...], (((1,), (1,)), ((), ())), preferred_element_type=F32
    )
    size = proj.shape[0] // parts
    pieces = [proj[k * size : (k + 1) * size] for k in range(parts)]
    for k, out in enumerate(proj_outs):
        out[...] = jnp.concatenate([pieces[j ^ k] for j in range(parts)], axis=0).astype(BF16)


def z_body(parts, *refs):
    rows_in, (in_proj, z_out) = refs[:parts], refs[parts:]
    z_out[...] = silu(jnp.dot(joined(rows_in), in_proj[1], preferred_element_type=F32))


def taps_out_body(rows, levels, stride, where, *refs):
    *taps, out = refs
    for index in range(taps[0].shape[0]):
        row = row_of(index, rows, levels, stride, where[0])
        for j, tap in enumerate(taps):
            out[row, j : j + 1, :] = tap[index : index + 1, :]


def ssm_body(first, parts, rows, levels, stride, *refs):
    where, prompts, near, far, act_in, z_in, dt_proj, dt_bias, a_log, d_skip, out_proj, before = (
        refs[:12]
    )
    outs, (after, y) = refs[12 : 12 + parts], refs[12 + parts :]
    rank = dt_proj.shape[0]
    states = a_log.shape[0]
    width = rank + 2 * states
    projected = near[:, :width].astype(F32) + far[:, :width].astype(F32)
    step_in = projected[:, :rank]
    high = step_in.astype(BF16)
    low = (step_in - high.astype(F32)).astype(BF16)
    delta = softplus(
        jnp.dot(high, dt_proj[...], preferred_element_type=F32)
        + jnp.dot(low, dt_proj[...], preferred_element_type=F32)
        + dt_bias[...]
    )
    maps = jnp.transpose(projected[:, rank:])
    act = act_in[...].astype(F32)
    driven = delta * act
    decay = -jnp.exp(a_log[...])
    for index in range(delta.shape[0]):
        row = row_of(index, rows, levels, stride, where[0])
        held_state = before[prompts[row]] if first else before[row]
        state = (
            jnp.exp(delta[index : index + 1, :] * decay) * held_state
            + driven[index : index + 1, :] * maps[:states, index : index + 1]
        )
        after[row] = state
        y[index : index + 1, :] = jnp.sum(
            state * maps[states:, index : index + 1], axis=0, keepdims=True
        )
    gated = ((y[...] + d_skip[...] * act) * z_in[...]).astype(BF16)
    mixed = jnp.dot(gated, out_proj[...], preferred_element_type=F32)
    size = mixed.shape[0] // parts
    for k, out in enumerate(outs):
        out[...] = mixed[k * size : (k + 1) * size].astype(BF16)


def route_body(near, far, x_in, gain, select, h_out, own_out, other_out):
    h = x_in[...] + (near[...].astype(F32) + far[...].astype(F32))
    h_out[...] = h
    routed = normalize(h, gain[...])
    picked = select[:, 0:1] * routed[0:1, :]
    for r in range(1, h.shape[0]):
        picked = picked + select[:, r : r + 1] * routed[r : r + 1, :]
    half = picked.shape[0] // 2
    own_out[...] = picked[:half].astype(BF16)
    other_out[...] = picked[half:].astype(BF16)


def expert_body(parts, *refs):
    rows_in, (gate, up, down) = refs[:parts], refs[parts : parts + 3]
    outs = refs[parts + 3 :]
    rows = joined(rows_in)
    dims = (((1,), (1,)), ((), ()))
    gate_val = lax.dot_general(rows, gate[...], dims, preferred_element_type=F32)
    up_val = lax.dot_general(rows, up[...], dims, preferred_element_type=F32)
    hidden = (silu(gate_val) * up_val).astype(BF16)
    result = jnp.dot(hidden, down[...], preferred_element_type=F32)
    size = result.shape[0] // parts
    for k, out in enumerate(outs):
        out[...] = result[k * size : (k + 1) * size].astype(BF16)


def combined(h_in, near, far, combine):
    half = far.shape[0]
    result = h_in[...]
    near_rows = near[...].astype(F32)
    far_rows = far[...].astype(F32)
    mixture = combine[:, 0:1] * near_rows[0:1, :]
    for s in range(1, half):
        mixture = mixture + combine[:, s : s + 1] * near_rows[s : s + 1, :]
    for s in range(half):
        mixture = mixture + combine[:, half + s : half + s + 1] * far_rows[s : s + 1, :]
    return (result + mixture).astype(BF16).astype(F32)


def store_own(out, rows, values, upper):
    @pl.when(upper == 0)
    def _():
        out[...] = values[:rows].astype(BF16)

    @pl.when(upper != 0)
    def _():
        out[...] = values[rows:].astype(BF16)


def next_body(where, h_in, near, far, combine, added, gain, out, x_out, normed_out):
    values = combined(h_in, near, far, combine)
    store_own(out, out.shape[0], values, where[1])
    x = values + added[...]
    x_out[...] = x
    normed_out[...] = normalize(x, gain[...]).astype(BF16)


def last_body(earlier, where, h_in, near, far, combine, *refs):
    before, out = refs[:earlier], refs[earlier]
    values = combined(h_in, near, far, combine)
    for step in range(earlier):
        out[step] = before[step][...]
    store_own(out.at[earlier], out.shape[1], values, where[1])


def on_device(
    layer_input,
    prompt_ssm,
    prompt_conv,
    sample_prompt,
    mamba_gain,
    in_proj,
    conv_weight,
    conv_bias,
    x_proj,
    dt_proj,
    dt_bias,
    a_log,
    d_skip,
    out_proj,
    moe_gain,
    route_ids,
    route_weights,
    w_gate,
    w_up,
    w_down,
):
    count = lax.axis_size("expert")
    levels, stride = levels_of(count)
    parts = levels[0][1] if levels else 1
    steps, rows, width = layer_input.shape
    group_rows = rows * count
    channels = in_proj.shape[2]
    taps = prompt_conv.shape[1]
    states = a_log.shape[0]
    slots = 2 * 2 * CAP
    me = lax.axis_index("expert")
    core = lax.axis_index("dp")
    where = jnp.stack([me, me // stride, core]).astype(jnp.int32)

    peer_input = partner(layer_input, stride, count)
    x, normed = call(
        start_body,
        "first_norm",
        [((2 * rows, width), F32), ((2 * rows, width), BF16)],
        [SMEM, ANY, VMEM, ANY],
        (where, in_hbm(layer_input), peer_input, in_hbm(mamba_gain.reshape(1, width))),
        scratch=[
            pltpu.VMEM(layer_input.shape, BF16),
            pltpu.VMEM((1, width), F32),
            pltpu.SemaphoreType.DMA((2,)),
        ],
    )
    mamba_gain = held(mamba_gain.reshape(1, width))
    moe_gain = held(moe_gain.reshape(1, width))
    normed, layer_input, prompt_ssm, prompt_conv, route_ids, route_weights = (
        lax.optimization_barrier(
            (normed, layer_input, prompt_ssm, prompt_conv, route_ids, route_weights)
        )
    )
    rows_in = spread(normed, levels, count)
    high = lax.reduce_precision(route_weights, 8, 7)
    routes = jnp.concatenate(
        [route_ids.astype(BF16), high.astype(BF16), (route_weights - high).astype(BF16)], axis=2
    ).reshape(-1)
    extra = -(-routes.size // group_rows)
    routes = other_core(routes)
    routes = jnp.pad(routes, (0, extra * group_rows - routes.size)).reshape(group_rows, extra)
    peer_ssm = other_core(prompt_ssm)
    peer_conv = other_core(prompt_conv)
    all_ssm = jnp.where(
        core == 0,
        jnp.concatenate([prompt_ssm, peer_ssm]),
        jnp.concatenate([peer_ssm, prompt_ssm]),
    )
    all_conv = jnp.where(
        core == 0,
        jnp.concatenate([prompt_conv, peer_conv]),
        jnp.concatenate([peer_conv, prompt_conv]),
    )
    conv_weight = held(conv_weight)
    conv_bias = held(conv_bias.reshape(1, channels))
    dt_bias = held(dt_bias.reshape(1, channels))
    d_skip = held(d_skip.reshape(1, channels))
    a_log = held(a_log)
    gate, up, down = w_gate[0], w_up[0], w_down[0]
    place = (rows, levels, stride)

    window = call(
        functools.partial(first_taps_body, *place),
        "first_taps",
        [((group_rows, channels), F32)] * taps,
        [SMEM, SMEM, VMEM],
        (where, sample_prompt, all_conv),
    )
    state = all_ssm
    outputs = []
    for step in range(steps):
        last = step == steps - 1
        if step == 0:
            rows_in, routes, window, state = lax.optimization_barrier(
                (rows_in, routes, window, state)
            )
        x_part, act, *proj = call(
            functools.partial(x_body, parts, taps),
            "mamba_x",
            [
                ((group_rows, channels), F32),
                ((group_rows, channels), BF16),
            ]
            + [((group_rows, x_proj.shape[0]), BF16)] * parts,
            [VMEM] * (parts + taps + 4),
            (*rows_in, *window, held(in_proj), conv_weight, conv_bias, held(x_proj)),
            flops=2 * group_rows * width * channels,
            moved=2 * width * channels,
        )
        window = [*window[1:], x_part]
        proj = add_everywhere(proj, levels, count)
        if step == 0:
            proj = jnp.concatenate([proj, routes], axis=1)
        proj, proj_far = back_from_halves(proj, stride, count)
        z_gate = call(
            functools.partial(z_body, parts),
            "mamba_z",
            [((group_rows, channels), F32)],
            [VMEM] * (parts + 1),
            (*rows_in, held(in_proj)),
            flops=2 * group_rows * width * channels,
            moved=2 * width * channels,
        )[0]
        if last:
            conv_state = call(
                functools.partial(taps_out_body, *place),
                "taps_out",
                [((group_rows, taps, channels), F32)],
                [SMEM] + [VMEM] * taps,
                (where, *window),
            )[0]
            proj_far, conv_state = lax.optimization_barrier((proj_far, conv_state))
        *mixed, state = call(
            functools.partial(ssm_body, step == 0, parts, *place),
            "mamba_ssm",
            [((group_rows // parts, width), BF16)] * parts
            + [((group_rows, states, channels), F32)],
            [SMEM, SMEM] + [VMEM] * 10,
            (
                where,
                sample_prompt,
                proj,
                proj_far,
                act,
                z_gate,
                held(dt_proj),
                dt_bias,
                a_log,
                d_skip,
                held(out_proj),
                state,
            ),
            scratch=[pltpu.VMEM((group_rows, channels), F32)],
            flops=2 * group_rows * width * channels,
            moved=2 * width * channels,
        )
        beside = (proj, proj_far, layer_input, peer_input) if step == 0 else ()
        mixed_near, beside = collect(mixed, levels, count, beside)
        if step == 0:
            near_routes, far_routes, later_own, later_peer = beside
            select, combine = call(
                functools.partial(table_body, steps, rows),
                "route_tables",
                [((steps, slots, 2 * rows), F32), ((steps, 2 * rows, slots), F32)],
                [SMEM, SMEM, SMEM],
                (
                    where,
                    near_routes[:, x_proj.shape[0] :].astype(F32).reshape(-1),
                    far_routes[:, x_proj.shape[0] :].astype(F32).reshape(-1),
                ),
            )
            later = call(
                functools.partial(later_body, steps),
                "later_inputs",
                [((2 * rows, width), F32)] * (steps - 1),
                [SMEM, VMEM, VMEM],
                (where, later_own, later_peer),
            )
        mixed_far = partner(mixed_near, stride, count)
        h, own, other = call(
            route_body,
            "route",
            [
                ((2 * rows, width), F32),
                ((slots // 2, width), BF16),
                ((slots // 2, width), BF16),
            ],
            [VMEM] * 5,
            (mixed_near, mixed_far, x, moe_gain, select[step]),
        )
        picked = spread(jnp.concatenate([own, other_core(other)]), levels, count)
        total_slots = slots * (count // 2)
        returned = call(
            functools.partial(expert_body, parts),
            "experts",
            [((total_slots // parts, width), BF16)] * parts,
            [VMEM] * (parts + 3),
            (*picked, held(gate), held(up), held(down)),
            flops=6 * total_slots * width * gate.shape[0],
            moved=6 * width * gate.shape[0],
        )
        out_near, _ = collect(returned, levels, count)
        summed = total([out_near, partner(out_near, stride, count)]).astype(BF16)
        out_far = other_core(summed[slots // 2 :])
        if last:
            layer_output = call(
                functools.partial(last_body, step),
                "last_output",
                [((steps, rows, width), BF16)],
                [SMEM] + [VMEM] * (4 + step),
                (where, h, summed, out_far, combine[step], *outputs),
            )[0]
        else:
            out, x, normed = call(
                next_body,
                "next_norm",
                [
                    ((rows, width), BF16),
                    ((2 * rows, width), F32),
                    ((2 * rows, width), BF16),
                ],
                [SMEM] + [VMEM] * 6,
                (where, h, summed, out_far, combine[step], later[step], mamba_gain),
            )
            outputs.append(out)
            rows_in = spread(normed, levels, count)
    return (layer_output, state, conv_state)


def solution(mesh):
    in_specs = (
        P(None, ("group", "dp", "expert"), None),
        P(("group", "dp"), None, "expert"),
        P(("group", "dp"), None, "expert"),
        P(("group", "dp")),
        P(),
        P(None, None, "expert"),
        P(None, "expert"),
        P("expert"),
        P(None, "expert"),
        P(None, "expert"),
        P("expert"),
        P(None, "expert"),
        P("expert"),
        P("expert", None),
        P(),
        P(None, ("group", "dp", "expert"), None),
        P(None, ("group", "dp", "expert"), None),
        P("dp", "expert", None),
        P("dp", "expert", None),
        P("dp", "expert", None),
    )
    out_specs = (
        P(None, ("group", "dp", "expert"), None),
        P(("group", "dp"), None, "expert"),
        P(("group", "dp"), None, "expert"),
    )
    return jax.shard_map(
        on_device, mesh=mesh, in_specs=in_specs, out_specs=out_specs, check_vma=False
    )
```

```python
import functools

import jax
import jax.numpy as jnp
from jax import lax
from jax.experimental import pallas as pl
from jax.experimental.pallas import tpu as pltpu
from jax.sharding import PartitionSpec as P

CAP = 2
EPS = 1e-05
MIB = 1 << 20
BESIDE = 10**10
F32 = jnp.float32
BF16 = jnp.bfloat16
VMEM = pl.BlockSpec(memory_space=pltpu.VMEM)
SMEM = pl.BlockSpec(memory_space=pltpu.SMEM)
ANY = pl.BlockSpec(memory_space=pl.ANY)


def silu(values):
    return values / (1.0 + jnp.exp(-values))


def softplus(values):
    return jnp.maximum(values, 0.0) + jnp.log1p(jnp.exp(-jnp.abs(values)))


def normalize(values, gain):
    return values * lax.rsqrt(jnp.mean(values * values, axis=-1, keepdims=True) + EPS) * gain


def held(array):
    return pltpu.with_memory_space_constraint(array, pltpu.VMEM)


def in_hbm(array):
    return pltpu.with_memory_space_constraint(array, pltpu.HBM)


def call(body, name, outs, specs, args, scratch=(), flops=BESIDE, moved=0, limit=8):
    return pl.pallas_call(
        body,
        name=name,
        out_shape=[jax.ShapeDtypeStruct(s, d) for s, d in outs],
        in_specs=specs,
        out_specs=[VMEM] * len(outs),
        scratch_shapes=list(scratch),
        cost_estimate=pl.CostEstimate(flops=flops, bytes_accessed=moved, transcendentals=0),
        compiler_params=pltpu.CompilerParams(vmem_limit_bytes=limit * MIB),
    )(*args)


def levels_of(count):
    levels, stride = [], 1
    while count // stride > 2:
        size = 4 if count // stride >= 8 else 2
        levels.append((stride, size))
        stride *= size
    return levels, stride


def partner(array, distance, count):
    return lax.ppermute(array, "expert", [(i, i ^ distance) for i in range(count)])


def other_core(array):
    return lax.ppermute(array, "dp", [(0, 1), (1, 0)])


def across(array, distance, count):
    pairs = [(i, count + (i ^ distance)) for i in range(count)]
    return lax.ppermute(array, ("dp", "expert"), pairs + [(b, a) for a, b in pairs])


def total(parts):
    result = parts[0].astype(F32)
    for part in parts[1:]:
        result = result + part.astype(F32)
    return result


def spread(block, levels, count):
    parts = [block]
    for position, (stride, size) in enumerate(reversed(levels)):
        whole = parts[0] if position == 0 else jnp.concatenate(parts, axis=0)
        parts = [whole] + [partner(whole, k * stride, count) for k in range(1, size)]
    return parts


def collect(parts, levels, count, beside=()):
    for position, (stride, size) in enumerate(levels):
        if position > 0:
            parts = jnp.split(parts, size, axis=0)
        parts = [parts[0]] + [partner(parts[k], k * stride, count) for k in range(1, size)]
        if position == 0 and beside:
            parts[1], beside = lax.optimization_barrier((parts[1], beside))
        parts = total(parts).astype(BF16)
    return parts, beside


def add_everywhere(parts, levels, count):
    for position, (stride, size) in enumerate(levels):
        if position == 0:
            parts = [across(parts[k], k * stride, count) for k in range(size)]
        else:
            rows, columns = parts.shape
            split = parts.reshape(stride, size, rows // (stride * size), columns)
            parts = [
                jnp.stack([split[:, j ^ k] for j in range(size)], axis=1).reshape(rows, columns)
                for k in range(size)
            ]
            parts = [parts[0]] + [partner(parts[k], k * stride, count) for k in range(1, size)]
        parts = total(parts).astype(BF16)
    return parts


def back_from_halves(array, stride, count):
    return across(array, 0, count), across(array, stride, count)


def joined(refs):
    if len(refs) == 1:
        return refs[0][...]
    return jnp.concatenate([r[...].astype(F32) for r in refs], axis=0).astype(BF16)


def place_rows(scratch, own, peer, upper):
    rows = own.shape[0]

    @pl.when(upper == 0)
    def _():
        scratch[0:rows, :] = own
        scratch[rows : 2 * rows, :] = peer

    @pl.when(upper != 0)
    def _():
        scratch[0:rows, :] = peer
        scratch[rows : 2 * rows, :] = own


def half_of(stride):
    return jnp.where(lax.axis_index("expert") >= stride, 1, 0)


def fetch_body(in_proj, own, gain, in_x_out, own_out, gain_out, arrived):
    copies = [
        pltpu.make_async_copy(in_proj.at[0], in_x_out, arrived.at[0]),
        pltpu.make_async_copy(own, own_out, arrived.at[1]),
        pltpu.make_async_copy(gain, gain_out, arrived.at[2]),
    ]
    for copy in copies:
        copy.start()
    for copy in copies:
        copy.wait()


def start_body(stride, own, peer, gain, x_out, normed_out):
    place_rows(x_out, own[0].astype(F32), peer[0].astype(F32), half_of(stride))
    normed_out[...] = normalize(x_out[...], gain[...]).astype(BF16)


def later_body(steps, stride, own, peer, *outs):
    for step in range(1, steps):
        place_rows(outs[step - 1], own[step].astype(F32), peer[step].astype(F32), half_of(stride))


def table_body(steps, rows, stride, own, peer, select_out, combine_out):
    upper = half_of(stride)
    core = lax.axis_index("dp")
    slots = 4 * CAP
    span = 2 * rows
    slot_a = lax.broadcasted_iota(jnp.int32, (slots, span), 0)
    row_a = lax.broadcasted_iota(jnp.int32, (slots, span), 1)
    row_b = lax.broadcasted_iota(jnp.int32, (span, slots), 0)
    slot_b = lax.broadcasted_iota(jnp.int32, (span, slots), 1)
    for step in range(steps):
        select = jnp.zeros((slots, span), F32)
        combine = jnp.zeros((span, slots), F32)
        for far in range(2):
            expert = (core if far == 0 else 1 - core).astype(F32)
            for block in range(2):
                count = jnp.int32(0)
                for j in range(rows):
                    at = (step * rows + j) * 6
                    entry = [
                        jnp.where(upper == block, own[at + m], peer[at + m]) for m in range(6)
                    ]
                    first = entry[0] == expert
                    second = entry[1] == expert
                    weight = jnp.where(first, entry[2] + entry[4], 0.0) + jnp.where(
                        second, entry[3] + entry[5], 0.0
                    )
                    named = jnp.where(first | second, 1, 0)
                    row = block * rows + j
                    slot = jnp.where(named == 1, (far * 2 + block) * CAP + count, -1)
                    select = jnp.where((slot_a == slot) & (row_a == row), 1.0, select)
                    combine = jnp.where((slot_b == slot) & (row_b == row), weight, combine)
                    count = count + named
        select_out[step] = select
        combine_out[step] = combine


def row_of(index, rows, levels, stride, me):
    within = index % rows
    half = (index // rows) % 2
    rest = index // (2 * rows)
    distance = 0
    for level_stride, size in reversed(levels):
        distance += (rest % size) * level_stride
        rest //= size
    return (((me ^ distance) & (stride - 1)) + half * stride) * rows + within


def first_state_body(rows, levels, stride, prompts, ssm, conv, state, *taps):
    me = lax.axis_index("expert")
    for index in range(taps[0].shape[0]):
        row = row_of(index, rows, levels, stride, me)
        prompt = prompts[row]
        state[row] = ssm[prompt]
        for j, tap in enumerate(taps):
            tap[index : index + 1, :] = conv[prompt, j : j + 1, :]


def x_body(parts, taps, *refs):
    rows_in, refs = refs[:parts], refs[parts:]
    held_taps, refs = refs[:taps], refs[taps:]
    in_proj, conv_weight, conv_bias, x_proj, x_out, act_out, *proj_outs = refs
    x_part = jnp.dot(joined(rows_in), in_proj[...], preferred_element_type=F32)
    x_out[...] = x_part
    mixed = x_part * conv_weight[taps : taps + 1, :]
    for j in range(taps):
        mixed = mixed + held_taps[j][...] * conv_weight[j : j + 1, :]
    act = silu(mixed + conv_bias[...]).astype(BF16)
    act_out[...] = act
    proj = lax.dot_general(
        act, x_proj[...], (((1,), (1,)), ((), ())), preferred_element_type=F32
    )
    size = proj.shape[0] // parts
    pieces = [proj[k * size : (k + 1) * size] for k in range(parts)]
    for k, out in enumerate(proj_outs):
        out[...] = jnp.concatenate([pieces[j ^ k] for j in range(parts)], axis=0).astype(BF16)


def z_body(parts, *refs):
    rows_in, (in_proj, z_out) = refs[:parts], refs[parts:]
    z_out[...] = silu(jnp.dot(joined(rows_in), in_proj[1], preferred_element_type=F32))


def taps_out_body(rows, levels, stride, *refs):
    *taps, out = refs
    me = lax.axis_index("expert")
    for index in range(taps[0].shape[0]):
        row = row_of(index, rows, levels, stride, me)
        for j, tap in enumerate(taps):
            out[row, j : j + 1, :] = tap[index : index + 1, :]


def ssm_body(parts, rows, levels, stride, *refs):
    near, far, act_in, z_in, dt_proj, dt_bias, a_log, d_skip, out_proj, before = refs[:10]
    outs, (after, y) = refs[10 : 10 + parts], refs[10 + parts :]
    me = lax.axis_index("expert")
    rank = dt_proj.shape[0]
    states = a_log.shape[0]
    width = rank + 2 * states
    projected = near[:, :width].astype(F32) + far[:, :width].astype(F32)
    step_in = projected[:, :rank]
    high = step_in.astype(BF16)
    low = (step_in - high.astype(F32)).astype(BF16)
    delta = softplus(
        jnp.dot(high, dt_proj[...], preferred_element_type=F32)
        + jnp.dot(low, dt_proj[...], preferred_element_type=F32)
        + dt_bias[...]
    )
    maps = jnp.transpose(projected[:, rank:])
    act = act_in[...].astype(F32)
    driven = delta * act
    decay = -jnp.exp(a_log[...])
    for index in range(delta.shape[0]):
        row = row_of(index, rows, levels, stride, me)
        state = (
            jnp.exp(delta[index : index + 1, :] * decay) * before[row]
            + driven[index : index + 1, :] * maps[:states, index : index + 1]
        )
        after[row] = state
        y[index : index + 1, :] = jnp.sum(
            state * maps[states:, index : index + 1], axis=0, keepdims=True
        )
    gated = ((y[...] + d_skip[...] * act) * z_in[...]).astype(BF16)
    mixed = jnp.dot(gated, out_proj[...], preferred_element_type=F32)
    size = mixed.shape[0] // parts
    for k, out in enumerate(outs):
        out[...] = mixed[k * size : (k + 1) * size].astype(BF16)


def route_body(near, far, x_in, gain, select, h_out, own_out, other_out):
    h = x_in[...] + (near[...].astype(F32) + far[...].astype(F32))
    h_out[...] = h
    routed = normalize(h, gain[...])
    picked = select[:, 0:1] * routed[0:1, :]
    for r in range(1, h.shape[0]):
        picked = picked + select[:, r : r + 1] * routed[r : r + 1, :]
    half = picked.shape[0] // 2
    own_out[...] = picked[:half].astype(BF16)
    other_out[...] = picked[half:].astype(BF16)


def expert_body(parts, *refs):
    rows_in, (gate, up, down) = refs[:parts], refs[parts : parts + 3]
    outs = refs[parts + 3 :]
    rows = joined(rows_in)
    dims = (((1,), (1,)), ((), ()))
    units = gate.shape[0]
    block = 128 if units % 128 == 0 else units
    hidden = []
    for start in range(0, units, block):
        some = slice(start, start + block)
        up_val = lax.dot_general(up[some, :], rows, dims, preferred_element_type=F32)
        gate_val = lax.dot_general(rows, gate[some, :], dims, preferred_element_type=F32)
        hidden.append((silu(gate_val) * jnp.transpose(up_val)).astype(BF16))
    hidden = hidden[0] if len(hidden) == 1 else jnp.concatenate(hidden, axis=1)
    result = jnp.dot(hidden, down[...], preferred_element_type=F32)
    size = result.shape[0] // parts
    for k, out in enumerate(outs):
        out[...] = result[k * size : (k + 1) * size].astype(BF16)


def combined(h_in, near, far, combine):
    half = far.shape[0]
    result = h_in[...]
    near_rows = near[...].astype(F32)
    far_rows = far[...].astype(F32)
    mixture = combine[:, 0:1] * near_rows[0:1, :]
    for s in range(1, half):
        mixture = mixture + combine[:, s : s + 1] * near_rows[s : s + 1, :]
    for s in range(half):
        mixture = mixture + combine[:, half + s : half + s + 1] * far_rows[s : s + 1, :]
    return (result + mixture).astype(BF16).astype(F32)


def store_own(out, rows, values, upper):
    @pl.when(upper == 0)
    def _():
        out[...] = values[:rows].astype(BF16)

    @pl.when(upper != 0)
    def _():
        out[...] = values[rows:].astype(BF16)


def next_body(stride, h_in, near, far, combine, added, gain, out, x_out, normed_out):
    values = combined(h_in, near, far, combine)
    store_own(out, out.shape[0], values, half_of(stride))
    x = values + added[...]
    x_out[...] = x
    normed_out[...] = normalize(x, gain[...]).astype(BF16)


def last_body(earlier, stride, h_in, near, far, combine, *refs):
    before, out = refs[:earlier], refs[earlier]
    values = combined(h_in, near, far, combine)
    for step in range(earlier):
        out[step] = before[step][...]
    store_own(out.at[earlier], out.shape[1], values, half_of(stride))


def on_device(
    layer_input,
    prompt_ssm,
    prompt_conv,
    sample_prompt,
    mamba_gain,
    in_proj,
    conv_weight,
    conv_bias,
    x_proj,
    dt_proj,
    dt_bias,
    a_log,
    d_skip,
    out_proj,
    moe_gain,
    route_ids,
    route_weights,
    w_gate,
    w_up,
    w_down,
):
    count = lax.axis_size("expert")
    levels, stride = levels_of(count)
    parts = levels[0][1] if levels else 1
    steps, rows, width = layer_input.shape
    group_rows = rows * count
    channels = in_proj.shape[2]
    taps = prompt_conv.shape[1]
    states = a_log.shape[0]
    slots = 2 * 2 * CAP
    core = lax.axis_index("dp")

    peer_input = partner(layer_input, stride, count)
    in_x, own_input, mamba_gain = call(
        fetch_body,
        "fetch",
        [((width, channels), BF16), (layer_input.shape, BF16), ((1, width), F32)],
        [ANY] * 3,
        (in_hbm(in_proj), in_hbm(layer_input), in_hbm(mamba_gain.reshape(1, width))),
        scratch=[pltpu.SemaphoreType.DMA((3,))],
        limit=16,
    )
    x, normed = call(
        functools.partial(start_body, stride),
        "first_norm",
        [((2 * rows, width), F32), ((2 * rows, width), BF16)],
        [VMEM] * 3,
        (own_input, peer_input, mamba_gain),
    )
    moe_gain = held(moe_gain.reshape(1, width))
    normed, layer_input, prompt_ssm, prompt_conv, route_ids, route_weights = (
        lax.optimization_barrier(
            (normed, layer_input, prompt_ssm, prompt_conv, route_ids, route_weights)
        )
    )
    rows_in = spread(normed, levels, count)
    high = lax.reduce_precision(route_weights, 8, 7)
    routes = jnp.concatenate(
        [route_ids.astype(BF16), high.astype(BF16), (route_weights - high).astype(BF16)], axis=2
    ).reshape(-1)
    extra = -(-routes.size // group_rows)
    routes = other_core(routes)
    routes = jnp.pad(routes, (0, extra * group_rows - routes.size)).reshape(group_rows, extra)
    peer_ssm = other_core(prompt_ssm)
    peer_conv = other_core(prompt_conv)
    all_ssm = jnp.where(
        core == 0,
        jnp.concatenate([prompt_ssm, peer_ssm]),
        jnp.concatenate([peer_ssm, prompt_ssm]),
    )
    all_conv = jnp.where(
        core == 0,
        jnp.concatenate([prompt_conv, peer_conv]),
        jnp.concatenate([peer_conv, prompt_conv]),
    )
    conv_weight = held(conv_weight)
    conv_bias = held(conv_bias.reshape(1, channels))
    dt_bias = held(dt_bias.reshape(1, channels))
    d_skip = held(d_skip.reshape(1, channels))
    a_log = held(a_log)
    gate, up, down = w_gate[0], w_up[0], w_down[0]
    place = (rows, levels, stride)

    state, *window = call(
        functools.partial(first_state_body, *place),
        "first_state",
        [((group_rows, states, channels), F32)] + [((group_rows, channels), F32)] * taps,
        [SMEM, VMEM, VMEM],
        (sample_prompt, all_ssm, all_conv),
    )
    outputs = []
    for step in range(steps):
        last = step == steps - 1
        if step == 0:
            rows_in, routes, window, state = lax.optimization_barrier(
                (rows_in, routes, window, state)
            )
        x_part, act, *proj = call(
            functools.partial(x_body, parts, taps),
            "mamba_x",
            [
                ((group_rows, channels), F32),
                ((group_rows, channels), BF16),
            ]
            + [((group_rows, x_proj.shape[0]), BF16)] * parts,
            [VMEM] * (parts + taps + 4),
            (*rows_in, *window, held(in_x), conv_weight, conv_bias, held(x_proj)),
        )
        window = [*window[1:], x_part]
        proj = add_everywhere(proj, levels, count)
        if step == 0:
            proj = jnp.concatenate([proj, routes], axis=1)
        proj, proj_far = back_from_halves(proj, stride, count)
        z_gate = call(
            functools.partial(z_body, parts),
            "mamba_z",
            [((group_rows, channels), F32)],
            [VMEM] * (parts + 1),
            (*rows_in, held(in_proj)),
        )[0]
        if last:
            conv_state = call(
                functools.partial(taps_out_body, *place),
                "taps_out",
                [((group_rows, taps, channels), F32)],
                [VMEM] * taps,
                (*window,),
            )[0]
            proj_far, conv_state = lax.optimization_barrier((proj_far, conv_state))
        *mixed, state = call(
            functools.partial(ssm_body, parts, *place),
            "mamba_ssm",
            [((group_rows // parts, width), BF16)] * parts
            + [((group_rows, states, channels), F32)],
            [VMEM] * 10,
            (
                proj,
                proj_far,
                act,
                z_gate,
                held(dt_proj),
                dt_bias,
                a_log,
                d_skip,
                held(out_proj),
                state,
            ),
            scratch=[pltpu.VMEM((group_rows, channels), F32)],
        )
        beside = (proj, proj_far, own_input, peer_input) if step == 0 else ()
        mixed_near, beside = collect(mixed, levels, count, beside)
        if step == 0:
            near_routes, far_routes, later_own, later_peer = beside
            select, combine = call(
                functools.partial(table_body, steps, rows, stride),
                "route_tables",
                [((steps, slots, 2 * rows), F32), ((steps, 2 * rows, slots), F32)],
                [SMEM, SMEM],
                (
                    near_routes[:, x_proj.shape[0] :].astype(F32).reshape(-1),
                    far_routes[:, x_proj.shape[0] :].astype(F32).reshape(-1),
                ),
            )
            later = call(
                functools.partial(later_body, steps, stride),
                "later_inputs",
                [((2 * rows, width), F32)] * (steps - 1),
                [VMEM, VMEM],
                (later_own, later_peer),
            )
        mixed_far = partner(mixed_near, stride, count)
        h, own, other = call(
            route_body,
            "route",
            [
                ((2 * rows, width), F32),
                ((slots // 2, width), BF16),
                ((slots // 2, width), BF16),
            ],
            [VMEM] * 5,
            (mixed_near, mixed_far, x, moe_gain, select[step]),
        )
        picked = spread(jnp.concatenate([own, other_core(other)]), levels, count)
        total_slots = slots * (count // 2)
        returned = call(
            functools.partial(expert_body, parts),
            "experts",
            [((total_slots // parts, width), BF16)] * parts,
            [VMEM] * (parts + 3),
            (*picked, held(gate), held(up), held(down)),
        )
        out_near, _ = collect(returned, levels, count)
        summed = total([out_near, partner(out_near, stride, count)]).astype(BF16)
        out_far = other_core(summed[slots // 2 :])
        if last:
            layer_output = call(
                functools.partial(last_body, step, stride),
                "last_output",
                [((steps, rows, width), BF16)],
                [VMEM] * (4 + step),
                (h, summed, out_far, combine[step], *outputs),
            )[0]
        else:
            out, x, normed = call(
                functools.partial(next_body, stride),
                "next_norm",
                [
                    ((rows, width), BF16),
                    ((2 * rows, width), F32),
                    ((2 * rows, width), BF16),
                ],
                [VMEM] * 6,
                (h, summed, out_far, combine[step], later[step], mamba_gain),
            )
            outputs.append(out)
            rows_in = spread(normed, levels, count)
    return (layer_output, state, conv_state)


def solution(mesh):
    in_specs = (
        P(None, ("group", "dp", "expert"), None),
        P(("group", "dp"), None, "expert"),
        P(("group", "dp"), None, "expert"),
        P(("group", "dp")),
        P(),
        P(None, None, "expert"),
        P(None, "expert"),
        P("expert"),
        P(None, "expert"),
        P(None, "expert"),
        P("expert"),
        P(None, "expert"),
        P("expert"),
        P("expert", None),
        P(),
        P(None, ("group", "dp", "expert"), None),
        P(None, ("group", "dp", "expert"), None),
        P("dp", "expert", None),
        P("dp", "expert", None),
        P("dp", "expert", None),
    )
    out_specs = (
        P(None, ("group", "dp", "expert"), None),
        P(("group", "dp"), None, "expert"),
        P(("group", "dp"), None, "expert"),
    )
    return jax.shard_map(
        on_device, mesh=mesh, in_specs=in_specs, out_specs=out_specs, check_vma=False
    )
```

```python
import functools

import jax
import jax.numpy as jnp
from jax import lax
from jax.experimental import pallas as pl
from jax.experimental.pallas import tpu as pltpu
from jax.sharding import PartitionSpec as P

CAP = 2
EPS = 1e-05
MIB = 1 << 20
BESIDE = 10**10
F32 = jnp.float32
BF16 = jnp.bfloat16
VMEM = pl.BlockSpec(memory_space=pltpu.VMEM)
SMEM = pl.BlockSpec(memory_space=pltpu.SMEM)
ANY = pl.BlockSpec(memory_space=pl.ANY)


def silu(values):
    return values / (1.0 + jnp.exp(-values))


def softplus(values):
    return jnp.maximum(values, 0.0) + jnp.log1p(jnp.exp(-jnp.abs(values)))


def normalize(values, gain):
    return values * lax.rsqrt(jnp.mean(values * values, axis=-1, keepdims=True) + EPS) * gain


def held(array):
    return pltpu.with_memory_space_constraint(array, pltpu.VMEM)


def in_hbm(array):
    return pltpu.with_memory_space_constraint(array, pltpu.HBM)


def call(body, name, outs, specs, args, scratch=(), flops=BESIDE, moved=0, limit=8):
    return pl.pallas_call(
        body,
        name=name,
        out_shape=[jax.ShapeDtypeStruct(s, d) for s, d in outs],
        in_specs=specs,
        out_specs=[VMEM] * len(outs),
        scratch_shapes=list(scratch),
        cost_estimate=pl.CostEstimate(flops=flops, bytes_accessed=moved, transcendentals=0),
        compiler_params=pltpu.CompilerParams(vmem_limit_bytes=limit * MIB),
    )(*args)


def levels_of(count):
    levels, stride = [], 1
    while count // stride > 2:
        size = 4 if count // stride >= 8 else 2
        levels.append((stride, size))
        stride *= size
    return levels, stride


def partner(array, distance, count):
    return lax.ppermute(array, "expert", [(i, i ^ distance) for i in range(count)])


def other_core(array):
    return lax.ppermute(array, "dp", [(0, 1), (1, 0)])


def across(array, distance, count):
    pairs = [(i, count + (i ^ distance)) for i in range(count)]
    return lax.ppermute(array, ("dp", "expert"), pairs + [(b, a) for a, b in pairs])


def total(parts):
    result = parts[0].astype(F32)
    for part in parts[1:]:
        result = result + part.astype(F32)
    return result


def spread(block, levels, count):
    parts = [block]
    for position, (stride, size) in enumerate(reversed(levels)):
        whole = parts[0] if position == 0 else jnp.concatenate(parts, axis=0)
        parts = [whole] + [partner(whole, k * stride, count) for k in range(1, size)]
    return parts


def collect(parts, levels, count, beside=()):
    for position, (stride, size) in enumerate(levels):
        if position > 0:
            parts = jnp.split(parts, size, axis=0)
        parts = [parts[0]] + [partner(parts[k], k * stride, count) for k in range(size - 1, 0, -1)]
        if position == 0 and beside:
            parts[1], beside = lax.optimization_barrier((parts[1], beside))
        parts = total(parts).astype(BF16)
    return parts, beside


def add_everywhere(parts, levels, count):
    for position, (stride, size) in enumerate(levels):
        if position == 0:
            parts = [across(parts[k], k * stride, count) for k in range(size - 1, -1, -1)]
        else:
            rows, columns = parts.shape
            split = parts.reshape(stride, size, rows // (stride * size), columns)
            parts = [
                jnp.stack([split[:, j ^ k] for j in range(size)], axis=1).reshape(rows, columns)
                for k in range(size)
            ]
            parts = [parts[0]] + [partner(parts[k], k * stride, count) for k in range(1, size)]
        parts = total(parts).astype(BF16)
    return parts


def back_from_halves(array, stride, count):
    return across(array, 0, count), across(array, stride, count)


def joined(refs):
    if len(refs) == 1:
        return refs[0][...]
    return jnp.concatenate([r[...].astype(F32) for r in refs], axis=0).astype(BF16)


def place_rows(scratch, own, peer, upper):
    rows = own.shape[0]

    @pl.when(upper == 0)
    def _():
        scratch[0:rows, :] = own
        scratch[rows : 2 * rows, :] = peer

    @pl.when(upper != 0)
    def _():
        scratch[0:rows, :] = peer
        scratch[rows : 2 * rows, :] = own


def half_of(stride):
    return jnp.where(lax.axis_index("expert") >= stride, 1, 0)


def fetch_body(in_proj, own, gain, in_x_out, own_out, gain_out, arrived):
    copies = [
        pltpu.make_async_copy(in_proj.at[0], in_x_out, arrived.at[0]),
        pltpu.make_async_copy(own, own_out, arrived.at[1]),
        pltpu.make_async_copy(gain, gain_out, arrived.at[2]),
    ]
    for copy in copies:
        copy.start()
    for copy in copies:
        copy.wait()


def start_body(stride, own, peer, gain, x_out, normed_out):
    place_rows(x_out, own[0].astype(F32), peer[0].astype(F32), half_of(stride))
    normed_out[...] = normalize(x_out[...], gain[...]).astype(BF16)


def later_body(steps, stride, own, peer, *outs):
    for step in range(1, steps):
        place_rows(outs[step - 1], own[step].astype(F32), peer[step].astype(F32), half_of(stride))


def table_body(steps, rows, stride, own, peer, select_out, combine_out):
    upper = half_of(stride)
    core = lax.axis_index("dp")
    slots = 4 * CAP
    span = 2 * rows
    slot_a = lax.broadcasted_iota(jnp.int32, (slots, span), 0)
    row_a = lax.broadcasted_iota(jnp.int32, (slots, span), 1)
    row_b = lax.broadcasted_iota(jnp.int32, (span, slots), 0)
    slot_b = lax.broadcasted_iota(jnp.int32, (span, slots), 1)
    for step in range(steps):
        select = jnp.zeros((slots, span), F32)
        combine = jnp.zeros((span, slots), F32)
        for far in range(2):
            expert = (core if far == 0 else 1 - core).astype(F32)
            for block in range(2):
                count = jnp.int32(0)
                for j in range(rows):
                    at = (step * rows + j) * 6
                    entry = [
                        jnp.where(upper == block, own[at + m], peer[at + m]) for m in range(6)
                    ]
                    first = entry[0] == expert
                    second = entry[1] == expert
                    weight = jnp.where(first, entry[2] + entry[4], 0.0) + jnp.where(
                        second, entry[3] + entry[5], 0.0
                    )
                    named = jnp.where(first | second, 1, 0)
                    row = block * rows + j
                    slot = jnp.where(named == 1, (far * 2 + block) * CAP + count, -1)
                    select = jnp.where((slot_a == slot) & (row_a == row), 1.0, select)
                    combine = jnp.where((slot_b == slot) & (row_b == row), weight, combine)
                    count = count + named
        select_out[step] = select
        combine_out[step] = combine


def row_of(index, rows, levels, stride, me):
    within = index % rows
    half = (index // rows) % 2
    rest = index // (2 * rows)
    distance = 0
    for level_stride, size in reversed(levels):
        distance += (rest % size) * level_stride
        rest //= size
    return (((me ^ distance) & (stride - 1)) + half * stride) * rows + within


def first_state_body(rows, levels, stride, prompts, ssm, conv, state, *taps):
    me = lax.axis_index("expert")
    for index in range(taps[0].shape[0]):
        row = row_of(index, rows, levels, stride, me)
        prompt = prompts[row]
        state[row] = ssm[prompt]
        for j, tap in enumerate(taps):
            tap[index : index + 1, :] = conv[prompt, j : j + 1, :]


def x_body(parts, taps, *refs):
    rows_in, refs = refs[:parts], refs[parts:]
    held_taps, refs = refs[:taps], refs[taps:]
    in_proj, conv_weight, conv_bias, x_proj, x_out, act_out, *proj_outs = refs
    weights = in_proj[...] if len(in_proj.shape) == 2 else in_proj[0]
    x_part = jnp.dot(joined(rows_in), weights, preferred_element_type=F32)
    x_out[...] = x_part
    mixed = x_part * conv_weight[taps : taps + 1, :]
    for j in range(taps):
        mixed = mixed + held_taps[j][...] * conv_weight[j : j + 1, :]
    act = silu(mixed + conv_bias[...]).astype(BF16)
    act_out[...] = act
    proj = lax.dot_general(
        act, x_proj[...], (((1,), (1,)), ((), ())), preferred_element_type=F32
    )
    size = proj.shape[0] // parts
    pieces = [proj[k * size : (k + 1) * size] for k in range(parts)]
    for k, out in enumerate(proj_outs):
        out[...] = jnp.concatenate([pieces[j ^ k] for j in range(parts)], axis=0).astype(BF16)


def z_body(parts, *refs):
    rows_in, (in_proj, z_out) = refs[:parts], refs[parts:]
    z_out[...] = silu(jnp.dot(joined(rows_in), in_proj[1], preferred_element_type=F32))


def taps_out_body(rows, levels, stride, *refs):
    *taps, out = refs
    me = lax.axis_index("expert")
    for index in range(taps[0].shape[0]):
        row = row_of(index, rows, levels, stride, me)
        for j, tap in enumerate(taps):
            out[row, j : j + 1, :] = tap[index : index + 1, :]


def ssm_body(parts, rows, levels, stride, *refs):
    near, far, act_in, z_in, dt_proj, dt_bias, a_log, d_skip, out_proj, before = refs[:10]
    outs, (after, y) = refs[10 : 10 + parts], refs[10 + parts :]
    me = lax.axis_index("expert")
    rank = dt_proj.shape[0]
    states = a_log.shape[0]
    width = rank + 2 * states
    projected = near[:, :width].astype(F32) + far[:, :width].astype(F32)
    step_in = projected[:, :rank]
    high = step_in.astype(BF16)
    low = (step_in - high.astype(F32)).astype(BF16)
    delta = softplus(
        jnp.dot(high, dt_proj[...], preferred_element_type=F32)
        + jnp.dot(low, dt_proj[...], preferred_element_type=F32)
        + dt_bias[...]
    )
    maps = jnp.transpose(projected[:, rank:])
    act = act_in[...].astype(F32)
    driven = delta * act
    decay = -jnp.exp(a_log[...])
    for index in range(delta.shape[0]):
        row = row_of(index, rows, levels, stride, me)
        state = (
            jnp.exp(delta[index : index + 1, :] * decay) * before[row]
            + driven[index : index + 1, :] * maps[:states, index : index + 1]
        )
        after[row] = state
        y[index : index + 1, :] = jnp.sum(
            state * maps[states:, index : index + 1], axis=0, keepdims=True
        )
    gated = ((y[...] + d_skip[...] * act) * z_in[...]).astype(BF16)
    mixed = jnp.dot(gated, out_proj[...], preferred_element_type=F32)
    size = mixed.shape[0] // parts
    for k, out in enumerate(outs):
        out[...] = mixed[k * size : (k + 1) * size].astype(BF16)


def route_body(near, far, x_in, gain, select, h_out, own_out, other_out):
    h = x_in[...] + (near[...].astype(F32) + far[...].astype(F32))
    h_out[...] = h
    routed = normalize(h, gain[...])
    picked = select[:, 0:1] * routed[0:1, :]
    for r in range(1, h.shape[0]):
        picked = picked + select[:, r : r + 1] * routed[r : r + 1, :]
    half = picked.shape[0] // 2
    own_out[...] = picked[:half].astype(BF16)
    other_out[...] = picked[half:].astype(BF16)


def expert_body(parts, *refs):
    rows_in, (gate, up, down) = refs[:parts], refs[parts : parts + 3]
    outs = refs[parts + 3 :]
    rows = joined(rows_in)
    dims = (((1,), (1,)), ((), ()))
    units = gate.shape[0]
    block = 128 if units % 128 == 0 else units
    hidden = []
    for start in range(0, units, block):
        some = slice(start, start + block)
        up_val = lax.dot_general(up[some, :], rows, dims, preferred_element_type=F32)
        gate_val = lax.dot_general(rows, gate[some, :], dims, preferred_element_type=F32)
        hidden.append((silu(gate_val) * jnp.transpose(up_val)).astype(BF16))
    hidden = hidden[0] if len(hidden) == 1 else jnp.concatenate(hidden, axis=1)
    result = jnp.dot(hidden, down[...], preferred_element_type=F32)
    size = result.shape[0] // parts
    for k, out in enumerate(outs):
        out[...] = result[k * size : (k + 1) * size].astype(BF16)


def combined(h_in, near, far, combine):
    half = far.shape[0]
    result = h_in[...]
    near_rows = near[...].astype(F32)
    far_rows = far[...].astype(F32)
    mixture = combine[:, 0:1] * near_rows[0:1, :]
    for s in range(1, half):
        mixture = mixture + combine[:, s : s + 1] * near_rows[s : s + 1, :]
    for s in range(half):
        mixture = mixture + combine[:, half + s : half + s + 1] * far_rows[s : s + 1, :]
    return (result + mixture).astype(BF16).astype(F32)


def store_own(out, rows, values, upper):
    @pl.when(upper == 0)
    def _():
        out[...] = values[:rows].astype(BF16)

    @pl.when(upper != 0)
    def _():
        out[...] = values[rows:].astype(BF16)


def next_body(stride, h_in, near, far, combine, added, gain, out, x_out, normed_out):
    values = combined(h_in, near, far, combine)
    store_own(out, out.shape[0], values, half_of(stride))
    x = values + added[...]
    x_out[...] = x
    normed_out[...] = normalize(x, gain[...]).astype(BF16)


def last_body(earlier, stride, h_in, near, far, combine, *refs):
    before, out = refs[:earlier], refs[earlier]
    values = combined(h_in, near, far, combine)
    for step in range(earlier):
        out[step] = before[step][...]
    store_own(out.at[earlier], out.shape[1], values, half_of(stride))


def on_device(
    layer_input,
    prompt_ssm,
    prompt_conv,
    sample_prompt,
    mamba_gain,
    in_proj,
    conv_weight,
    conv_bias,
    x_proj,
    dt_proj,
    dt_bias,
    a_log,
    d_skip,
    out_proj,
    moe_gain,
    route_ids,
    route_weights,
    w_gate,
    w_up,
    w_down,
):
    count = lax.axis_size("expert")
    levels, stride = levels_of(count)
    parts = levels[0][1] if levels else 1
    steps, rows, width = layer_input.shape
    group_rows = rows * count
    channels = in_proj.shape[2]
    taps = prompt_conv.shape[1]
    states = a_log.shape[0]
    slots = 2 * 2 * CAP
    core = lax.axis_index("dp")

    peer_input = partner(layer_input, stride, count)
    in_x, own_input, mamba_gain = call(
        fetch_body,
        "fetch",
        [((width, channels), BF16), (layer_input.shape, BF16), ((1, width), F32)],
        [ANY] * 3,
        (in_hbm(in_proj), in_hbm(layer_input), in_hbm(mamba_gain.reshape(1, width))),
        scratch=[pltpu.SemaphoreType.DMA((3,))],
        limit=16,
    )
    x, normed = call(
        functools.partial(start_body, stride),
        "first_norm",
        [((2 * rows, width), F32), ((2 * rows, width), BF16)],
        [VMEM] * 3,
        (own_input, peer_input, mamba_gain),
    )
    moe_gain = held(moe_gain.reshape(1, width))
    normed, layer_input, prompt_ssm, prompt_conv, route_ids, route_weights = (
        lax.optimization_barrier(
            (normed, layer_input, prompt_ssm, prompt_conv, route_ids, route_weights)
        )
    )
    rows_in = spread(normed, levels, count)
    high = lax.reduce_precision(route_weights, 8, 7)
    routes = jnp.concatenate(
        [route_ids.astype(BF16), high.astype(BF16), (route_weights - high).astype(BF16)], axis=2
    ).reshape(-1)
    extra = -(-routes.size // group_rows)
    routes = other_core(routes)
    routes = jnp.pad(routes, (0, extra * group_rows - routes.size)).reshape(group_rows, extra)
    peer_ssm = other_core(prompt_ssm)
    peer_conv = other_core(prompt_conv)
    all_ssm = jnp.where(
        core == 0,
        jnp.concatenate([prompt_ssm, peer_ssm]),
        jnp.concatenate([peer_ssm, prompt_ssm]),
    )
    all_conv = jnp.where(
        core == 0,
        jnp.concatenate([prompt_conv, peer_conv]),
        jnp.concatenate([peer_conv, prompt_conv]),
    )
    conv_weight = held(conv_weight)
    conv_bias = held(conv_bias.reshape(1, channels))
    dt_bias = held(dt_bias.reshape(1, channels))
    d_skip = held(d_skip.reshape(1, channels))
    a_log = held(a_log)
    gate, up, down = w_gate[0], w_up[0], w_down[0]
    place = (rows, levels, stride)

    state, *window = call(
        functools.partial(first_state_body, *place),
        "first_state",
        [((group_rows, states, channels), F32)] + [((group_rows, channels), F32)] * taps,
        [SMEM, VMEM, VMEM],
        (sample_prompt, all_ssm, all_conv),
    )
    outputs = []
    for step in range(steps):
        last = step == steps - 1
        if step == 0:
            rows_in, routes, window, state = lax.optimization_barrier(
                (rows_in, routes, window, state)
            )
        x_part, act, *proj = call(
            functools.partial(x_body, parts, taps),
            "mamba_x",
            [
                ((group_rows, channels), F32),
                ((group_rows, channels), BF16),
            ]
            + [((group_rows, x_proj.shape[0]), BF16)] * parts,
            [VMEM] * (parts + taps + 4),
            (
                *rows_in,
                *window,
                held(in_x if step == 0 else in_proj),
                conv_weight,
                conv_bias,
                held(x_proj),
            ),
        )
        window = [*window[1:], x_part]
        proj = add_everywhere(proj, levels, count)
        if step == 0:
            proj = jnp.concatenate([proj, routes], axis=1)
        proj, proj_far = back_from_halves(proj, stride, count)
        z_gate = call(
            functools.partial(z_body, parts),
            "mamba_z",
            [((group_rows, channels), F32)],
            [VMEM] * (parts + 1),
            (*rows_in, held(in_proj)),
        )[0]
        if last:
            conv_state = call(
                functools.partial(taps_out_body, *place),
                "taps_out",
                [((group_rows, taps, channels), F32)],
                [VMEM] * taps,
                (*window,),
            )[0]
            proj_far, conv_state = lax.optimization_barrier((proj_far, conv_state))
        *mixed, state = call(
            functools.partial(ssm_body, parts, *place),
            "mamba_ssm",
            [((group_rows // parts, width), BF16)] * parts
            + [((group_rows, states, channels), F32)],
            [VMEM] * 10,
            (
                proj,
                proj_far,
                act,
                z_gate,
                held(dt_proj),
                dt_bias,
                a_log,
                d_skip,
                held(out_proj),
                state,
            ),
            scratch=[pltpu.VMEM((group_rows, channels), F32)],
        )
        beside = (proj, proj_far, own_input, peer_input) if step == 0 else ()
        mixed_near, beside = collect(mixed, levels, count, beside)
        if step == 0:
            near_routes, far_routes, later_own, later_peer = beside
            select, combine = call(
                functools.partial(table_body, steps, rows, stride),
                "route_tables",
                [((steps, slots, 2 * rows), F32), ((steps, 2 * rows, slots), F32)],
                [SMEM, SMEM],
                (
                    near_routes[:, x_proj.shape[0] :].astype(F32).reshape(-1),
                    far_routes[:, x_proj.shape[0] :].astype(F32).reshape(-1),
                ),
            )
            later = call(
                functools.partial(later_body, steps, stride),
                "later_inputs",
                [((2 * rows, width), F32)] * (steps - 1),
                [VMEM, VMEM],
                (later_own, later_peer),
            )
        mixed_far = partner(mixed_near, stride, count)
        h, own, other = call(
            route_body,
            "route",
            [
                ((2 * rows, width), F32),
                ((slots // 2, width), BF16),
                ((slots // 2, width), BF16),
            ],
            [VMEM] * 5,
            (mixed_near, mixed_far, x, moe_gain, select[step]),
        )
        picked = spread(jnp.concatenate([own, other_core(other)]), levels, count)
        total_slots = slots * (count // 2)
        returned = call(
            functools.partial(expert_body, parts),
            "experts",
            [((total_slots // parts, width), BF16)] * parts,
            [VMEM] * (parts + 3),
            (*picked, held(gate), held(up), held(down)),
        )
        out_near, _ = collect(returned, levels, count)
        summed = total([out_near, partner(out_near, stride, count)]).astype(BF16)
        out_far = other_core(summed[slots // 2 :])
        if last:
            layer_output = call(
                functools.partial(last_body, step, stride),
                "last_output",
                [((steps, rows, width), BF16)],
                [VMEM] * (4 + step),
                (h, summed, out_far, combine[step], *outputs),
            )[0]
        else:
            out, x, normed = call(
                functools.partial(next_body, stride),
                "next_norm",
                [
                    ((rows, width), BF16),
                    ((2 * rows, width), F32),
                    ((2 * rows, width), BF16),
                ],
                [VMEM] * 6,
                (h, summed, out_far, combine[step], later[step], mamba_gain),
            )
            outputs.append(out)
            rows_in = spread(normed, levels, count)
    return (layer_output, state, conv_state)


def solution(mesh):
    in_specs = (
        P(None, ("group", "dp", "expert"), None),
        P(("group", "dp"), None, "expert"),
        P(("group", "dp"), None, "expert"),
        P(("group", "dp")),
        P(),
        P(None, None, "expert"),
        P(None, "expert"),
        P("expert"),
        P(None, "expert"),
        P(None, "expert"),
        P("expert"),
        P(None, "expert"),
        P("expert"),
        P("expert", None),
        P(),
        P(None, ("group", "dp", "expert"), None),
        P(None, ("group", "dp", "expert"), None),
        P("dp", "expert", None),
        P("dp", "expert", None),
        P("dp", "expert", None),
    )
    out_specs = (
        P(None, ("group", "dp", "expert"), None),
        P(("group", "dp"), None, "expert"),
        P(("group", "dp"), None, "expert"),
    )
    return jax.shard_map(
        on_device, mesh=mesh, in_specs=in_specs, out_specs=out_specs, check_vma=False
    )
```

```python
import functools

import jax
import jax.numpy as jnp
from jax import lax
from jax.experimental import pallas as pl
from jax.experimental.pallas import tpu as pltpu
from jax.sharding import PartitionSpec as P

CAP = 2
EPS = 1e-05
MIB = 1 << 20
BESIDE = 10**10
F32 = jnp.float32
BF16 = jnp.bfloat16
VMEM = pl.BlockSpec(memory_space=pltpu.VMEM)
SMEM = pl.BlockSpec(memory_space=pltpu.SMEM)
ANY = pl.BlockSpec(memory_space=pl.ANY)


def silu(values):
    return values / (1.0 + jnp.exp(-values))


def softplus(values):
    return jnp.maximum(values, 0.0) + jnp.log1p(jnp.exp(-jnp.abs(values)))


def normalize(values, gain):
    return values * lax.rsqrt(jnp.mean(values * values, axis=-1, keepdims=True) + EPS) * gain


def held(array):
    return pltpu.with_memory_space_constraint(array, pltpu.VMEM)


def in_hbm(array):
    return pltpu.with_memory_space_constraint(array, pltpu.HBM)


def call(body, name, outs, specs, args, scratch=(), flops=BESIDE, moved=0, limit=8):
    return pl.pallas_call(
        body,
        name=name,
        out_shape=[jax.ShapeDtypeStruct(s, d) for s, d in outs],
        in_specs=specs,
        out_specs=[VMEM] * len(outs),
        scratch_shapes=list(scratch),
        cost_estimate=pl.CostEstimate(flops=flops, bytes_accessed=moved, transcendentals=0),
        compiler_params=pltpu.CompilerParams(vmem_limit_bytes=limit * MIB),
    )(*args)


def levels_of(count):
    levels, stride = [], 1
    while count // stride > 2:
        size = 4 if count // stride >= 8 else 2
        levels.append((stride, size))
        stride *= size
    return levels, stride


def partner(array, distance, count):
    return lax.ppermute(array, "expert", [(i, i ^ distance) for i in range(count)])


def other_core(array):
    return lax.ppermute(array, "dp", [(0, 1), (1, 0)])


def across(array, distance, count):
    pairs = [(i, count + (i ^ distance)) for i in range(count)]
    return lax.ppermute(array, ("dp", "expert"), pairs + [(b, a) for a, b in pairs])


def total(parts):
    result = parts[0].astype(F32)
    for part in parts[1:]:
        result = result + part.astype(F32)
    return result


def spread(block, levels, count):
    parts = [block]
    for position, (stride, size) in enumerate(reversed(levels)):
        whole = parts[0] if position == 0 else jnp.concatenate(parts, axis=0)
        parts = [whole] + [partner(whole, k * stride, count) for k in range(1, size)]
    return parts


def collect(parts, levels, count, beside=()):
    for position, (stride, size) in enumerate(levels):
        if position > 0:
            parts = jnp.split(parts, size, axis=0)
        parts = [parts[0]] + [partner(parts[k], k * stride, count) for k in range(size - 1, 0, -1)]
        if position == 0 and beside:
            parts[1], beside = lax.optimization_barrier((parts[1], beside))
        parts = total(parts).astype(BF16)
    return parts, beside


def add_everywhere(parts, levels, count):
    for position, (stride, size) in enumerate(levels):
        if position == 0:
            parts = [across(parts[k], k * stride, count) for k in range(size - 1, -1, -1)]
        else:
            rows, columns = parts.shape
            split = parts.reshape(stride, size, rows // (stride * size), columns)
            parts = [
                jnp.stack([split[:, j ^ k] for j in range(size)], axis=1).reshape(rows, columns)
                for k in range(size)
            ]
            parts = [parts[0]] + [partner(parts[k], k * stride, count) for k in range(1, size)]
        parts = total(parts).astype(BF16)
    return parts


def back_from_halves(array, stride, count):
    return across(array, 0, count), across(array, stride, count)


def joined(refs):
    if len(refs) == 1:
        return refs[0][...]
    return jnp.concatenate([r[...].astype(F32) for r in refs], axis=0).astype(BF16)


def place_rows(scratch, own, peer, upper):
    rows = own.shape[0]

    @pl.when(upper == 0)
    def _():
        scratch[0:rows, :] = own
        scratch[rows : 2 * rows, :] = peer

    @pl.when(upper != 0)
    def _():
        scratch[0:rows, :] = peer
        scratch[rows : 2 * rows, :] = own


def half_of(stride):
    return jnp.where(lax.axis_index("expert") >= stride, 1, 0)


def fetch_body(in_proj, own, gain, in_x_out, own_out, gain_out, arrived):
    copies = [
        pltpu.make_async_copy(in_proj.at[0], in_x_out, arrived.at[0]),
        pltpu.make_async_copy(own, own_out, arrived.at[1]),
        pltpu.make_async_copy(gain, gain_out, arrived.at[2]),
    ]
    for copy in copies:
        copy.start()
    for copy in copies:
        copy.wait()


def start_body(stride, own, peer, gain, x_out, normed_out):
    place_rows(x_out, own[0].astype(F32), peer[0].astype(F32), half_of(stride))
    normed_out[...] = normalize(x_out[...], gain[...]).astype(BF16)


def later_body(steps, stride, own, peer, *outs):
    for step in range(1, steps):
        place_rows(outs[step - 1], own[step].astype(F32), peer[step].astype(F32), half_of(stride))


def table_body(steps, rows, stride, own, peer, select_out, combine_out):
    upper = half_of(stride)
    core = lax.axis_index("dp")
    slots = 4 * CAP
    span = 2 * rows
    slot_a = lax.broadcasted_iota(jnp.int32, (slots, span), 0)
    row_a = lax.broadcasted_iota(jnp.int32, (slots, span), 1)
    row_b = lax.broadcasted_iota(jnp.int32, (span, slots), 0)
    slot_b = lax.broadcasted_iota(jnp.int32, (span, slots), 1)
    for step in range(steps):
        select = jnp.zeros((slots, span), F32)
        combine = jnp.zeros((span, slots), F32)
        for far in range(2):
            expert = (core if far == 0 else 1 - core).astype(F32)
            for block in range(2):
                count = jnp.int32(0)
                for j in range(rows):
                    at = (step * rows + j) * 6
                    entry = [
                        jnp.where(upper == block, own[at + m], peer[at + m]) for m in range(6)
                    ]
                    first = entry[0] == expert
                    second = entry[1] == expert
                    weight = jnp.where(first, entry[2] + entry[4], 0.0) + jnp.where(
                        second, entry[3] + entry[5], 0.0
                    )
                    named = jnp.where(first | second, 1, 0)
                    row = block * rows + j
                    slot = jnp.where(named == 1, (far * 2 + block) * CAP + count, -1)
                    select = jnp.where((slot_a == slot) & (row_a == row), 1.0, select)
                    combine = jnp.where((slot_b == slot) & (row_b == row), weight, combine)
                    count = count + named
        select_out[step] = select
        combine_out[step] = combine


def row_of(index, rows, levels, stride, me):
    within = index % rows
    half = (index // rows) % 2
    rest = index // (2 * rows)
    distance = 0
    for level_stride, size in reversed(levels):
        distance += (rest % size) * level_stride
        rest //= size
    return (((me ^ distance) & (stride - 1)) + half * stride) * rows + within


def first_state_body(rows, levels, stride, prompts, ssm, conv, state, *taps):
    me = lax.axis_index("expert")
    for index in range(taps[0].shape[0]):
        row = row_of(index, rows, levels, stride, me)
        prompt = prompts[row]
        state[row] = ssm[prompt]
        for j, tap in enumerate(taps):
            tap[index : index + 1, :] = conv[prompt, j : j + 1, :]


def x_body(parts, taps, *refs):
    rows_in, refs = refs[:parts], refs[parts:]
    held_taps, refs = refs[:taps], refs[taps:]
    in_proj, conv_weight, conv_bias, x_proj, x_out, act_out, *proj_outs = refs
    weights = in_proj[...] if len(in_proj.shape) == 2 else in_proj[0]
    x_part = jnp.dot(joined(rows_in), weights, preferred_element_type=F32)
    x_out[...] = x_part
    mixed = x_part * conv_weight[taps : taps + 1, :]
    for j in range(taps):
        mixed = mixed + held_taps[j][...] * conv_weight[j : j + 1, :]
    act = silu(mixed + conv_bias[...]).astype(BF16)
    act_out[...] = act
    proj = lax.dot_general(
        act, x_proj[...], (((1,), (1,)), ((), ())), preferred_element_type=F32
    )
    size = proj.shape[0] // parts
    pieces = [proj[k * size : (k + 1) * size] for k in range(parts)]
    for k, out in enumerate(proj_outs):
        out[...] = jnp.concatenate([pieces[j ^ k] for j in range(parts)], axis=0).astype(BF16)


def z_body(parts, *refs):
    rows_in, (in_proj, z_out) = refs[:parts], refs[parts:]
    z_out[...] = silu(jnp.dot(joined(rows_in), in_proj[1], preferred_element_type=F32))


def taps_out_body(rows, levels, stride, *refs):
    *taps, out = refs
    me = lax.axis_index("expert")
    for index in range(taps[0].shape[0]):
        row = row_of(index, rows, levels, stride, me)
        for j, tap in enumerate(taps):
            out[row, j : j + 1, :] = tap[index : index + 1, :]


def ssm_body(parts, rows, levels, stride, *refs):
    near, far, act_in, z_in, dt_proj, dt_bias, a_log, d_skip, out_proj, before = refs[:10]
    outs, (after, y) = refs[10 : 10 + parts], refs[10 + parts :]
    me = lax.axis_index("expert")
    rank = dt_proj.shape[0]
    states = a_log.shape[0]
    width = rank + 2 * states
    projected = near[:, :width].astype(F32) + far[:, :width].astype(F32)
    step_in = projected[:, :rank]
    high = step_in.astype(BF16)
    low = (step_in - high.astype(F32)).astype(BF16)
    delta = softplus(
        jnp.dot(high, dt_proj[...], preferred_element_type=F32)
        + jnp.dot(low, dt_proj[...], preferred_element_type=F32)
        + dt_bias[...]
    )
    maps = jnp.transpose(projected[:, rank:])
    act = act_in[...].astype(F32)
    driven = delta * act
    decay = -jnp.exp(a_log[...])
    for index in range(delta.shape[0]):
        row = row_of(index, rows, levels, stride, me)
        state = (
            jnp.exp(delta[index : index + 1, :] * decay) * before[row]
            + driven[index : index + 1, :] * maps[:states, index : index + 1]
        )
        after[row] = state
        y[index : index + 1, :] = jnp.sum(
            state * maps[states:, index : index + 1], axis=0, keepdims=True
        )
    gated = ((y[...] + d_skip[...] * act) * z_in[...]).astype(BF16)
    mixed = jnp.dot(gated, out_proj[...], preferred_element_type=F32)
    size = mixed.shape[0] // parts
    for k, out in enumerate(outs):
        out[...] = mixed[k * size : (k + 1) * size].astype(BF16)


def route_body(near, far, x_in, gain, select, h_out, own_out, other_out):
    h = x_in[...] + (near[...].astype(F32) + far[...].astype(F32))
    h_out[...] = h
    routed = normalize(h, gain[...])
    picked = select[:, 0:1] * routed[0:1, :]
    for r in range(1, h.shape[0]):
        picked = picked + select[:, r : r + 1] * routed[r : r + 1, :]
    half = picked.shape[0] // 2
    own_out[...] = picked[:half].astype(BF16)
    other_out[...] = picked[half:].astype(BF16)


def expert_body(parts, *refs):
    rows_in, (gate, up, down) = refs[:parts], refs[parts : parts + 3]
    outs = refs[parts + 3 :]
    rows = joined(rows_in)
    dims = (((1,), (1,)), ((), ()))
    units = gate.shape[0]
    block = 128 if units % 128 == 0 else units
    hidden = []
    for start in range(0, units, block):
        some = slice(start, start + block)
        up_val = lax.dot_general(up[some, :], rows, dims, preferred_element_type=F32)
        gate_val = lax.dot_general(rows, gate[some, :], dims, preferred_element_type=F32)
        hidden.append((silu(gate_val) * jnp.transpose(up_val)).astype(BF16))
    hidden = hidden[0] if len(hidden) == 1 else jnp.concatenate(hidden, axis=1)
    result = jnp.dot(hidden, down[...], preferred_element_type=F32)
    size = result.shape[0] // parts
    for k, out in enumerate(outs):
        out[...] = result[k * size : (k + 1) * size].astype(BF16)


def combined(h_in, near, far, combine):
    half = far.shape[0]
    result = h_in[...]
    near_rows = near[...].astype(F32)
    far_rows = far[...].astype(F32)
    mixture = combine[:, 0:1] * near_rows[0:1, :]
    for s in range(1, half):
        mixture = mixture + combine[:, s : s + 1] * near_rows[s : s + 1, :]
    for s in range(half):
        mixture = mixture + combine[:, half + s : half + s + 1] * far_rows[s : s + 1, :]
    return (result + mixture).astype(BF16).astype(F32)


def store_own(out, rows, values, upper):
    @pl.when(upper == 0)
    def _():
        out[...] = values[:rows].astype(BF16)

    @pl.when(upper != 0)
    def _():
        out[...] = values[rows:].astype(BF16)


def next_body(stride, h_in, near, far, combine, added, gain, out, x_out, normed_out):
    values = combined(h_in, near, far, combine)
    store_own(out, out.shape[0], values, half_of(stride))
    x = values + added[...]
    x_out[...] = x
    normed_out[...] = normalize(x, gain[...]).astype(BF16)


def last_body(earlier, stride, h_in, near, far, combine, *refs):
    before, out = refs[:earlier], refs[earlier]
    values = combined(h_in, near, far, combine)
    for step in range(earlier):
        out[step] = before[step][...]
    store_own(out.at[earlier], out.shape[1], values, half_of(stride))


def on_device(
    layer_input,
    prompt_ssm,
    prompt_conv,
    sample_prompt,
    mamba_gain,
    in_proj,
    conv_weight,
    conv_bias,
    x_proj,
    dt_proj,
    dt_bias,
    a_log,
    d_skip,
    out_proj,
    moe_gain,
    route_ids,
    route_weights,
    w_gate,
    w_up,
    w_down,
):
    count = lax.axis_size("expert")
    levels, stride = levels_of(count)
    parts = levels[0][1] if levels else 1
    steps, rows, width = layer_input.shape
    group_rows = rows * count
    channels = in_proj.shape[2]
    taps = prompt_conv.shape[1]
    states = a_log.shape[0]
    slots = 2 * 2 * CAP
    core = lax.axis_index("dp")

    peer_input = partner(layer_input, stride, count)
    in_x, own_input, mamba_gain = call(
        fetch_body,
        "fetch",
        [((width, channels), BF16), (layer_input.shape, BF16), ((1, width), F32)],
        [ANY] * 3,
        (in_hbm(in_proj), in_hbm(layer_input), in_hbm(mamba_gain.reshape(1, width))),
        scratch=[pltpu.SemaphoreType.DMA((3,))],
        limit=16,
    )
    x, normed = call(
        functools.partial(start_body, stride),
        "first_norm",
        [((2 * rows, width), F32), ((2 * rows, width), BF16)],
        [VMEM] * 3,
        (own_input, peer_input, mamba_gain),
    )
    moe_gain = held(moe_gain.reshape(1, width))
    in_x, prompt_ssm, prompt_conv = lax.optimization_barrier((in_x, prompt_ssm, prompt_conv))
    normed, route_ids, route_weights = lax.optimization_barrier(
        (normed, route_ids, route_weights)
    )
    rows_in = spread(normed, levels, count)
    high = lax.reduce_precision(route_weights, 8, 7)
    routes = jnp.concatenate(
        [route_ids.astype(BF16), high.astype(BF16), (route_weights - high).astype(BF16)], axis=2
    ).reshape(-1)
    extra = -(-routes.size // group_rows)
    routes = other_core(routes)
    routes = jnp.pad(routes, (0, extra * group_rows - routes.size)).reshape(group_rows, extra)
    peer_ssm = other_core(prompt_ssm)
    peer_conv = other_core(prompt_conv)
    all_ssm = jnp.where(
        core == 0,
        jnp.concatenate([prompt_ssm, peer_ssm]),
        jnp.concatenate([peer_ssm, prompt_ssm]),
    )
    all_conv = jnp.where(
        core == 0,
        jnp.concatenate([prompt_conv, peer_conv]),
        jnp.concatenate([peer_conv, prompt_conv]),
    )
    conv_weight = held(conv_weight)
    conv_bias = held(conv_bias.reshape(1, channels))
    dt_bias = held(dt_bias.reshape(1, channels))
    d_skip = held(d_skip.reshape(1, channels))
    a_log = held(a_log)
    gate, up, down = w_gate[0], w_up[0], w_down[0]
    place = (rows, levels, stride)

    state, *window = call(
        functools.partial(first_state_body, *place),
        "first_state",
        [((group_rows, states, channels), F32)] + [((group_rows, channels), F32)] * taps,
        [SMEM, VMEM, VMEM],
        (sample_prompt, all_ssm, all_conv),
    )
    outputs = []
    for step in range(steps):
        last = step == steps - 1
        if step == 0:
            rows_in, routes, window, state = lax.optimization_barrier(
                (rows_in, routes, window, state)
            )
        x_part, act, *proj = call(
            functools.partial(x_body, parts, taps),
            "mamba_x",
            [
                ((group_rows, channels), F32),
                ((group_rows, channels), BF16),
            ]
            + [((group_rows, x_proj.shape[0]), BF16)] * parts,
            [VMEM] * (parts + taps + 4),
            (
                *rows_in,
                *window,
                held(in_x if step == 0 else in_proj),
                conv_weight,
                conv_bias,
                held(x_proj),
            ),
        )
        window = [*window[1:], x_part]
        proj = add_everywhere(proj, levels, count)
        if step == 0:
            proj = jnp.concatenate([proj, routes], axis=1)
        proj, proj_far = back_from_halves(proj, stride, count)
        z_gate = call(
            functools.partial(z_body, parts),
            "mamba_z",
            [((group_rows, channels), F32)],
            [VMEM] * (parts + 1),
            (*rows_in, held(in_proj)),
        )[0]
        if last:
            conv_state = call(
                functools.partial(taps_out_body, *place),
                "taps_out",
                [((group_rows, taps, channels), F32)],
                [VMEM] * taps,
                (*window,),
            )[0]
            proj_far, conv_state = lax.optimization_barrier((proj_far, conv_state))
        *mixed, state = call(
            functools.partial(ssm_body, parts, *place),
            "mamba_ssm",
            [((group_rows // parts, width), BF16)] * parts
            + [((group_rows, states, channels), F32)],
            [VMEM] * 10,
            (
                proj,
                proj_far,
                act,
                z_gate,
                held(dt_proj),
                dt_bias,
                a_log,
                d_skip,
                held(out_proj),
                state,
            ),
            scratch=[pltpu.VMEM((group_rows, channels), F32)],
        )
        beside = (proj, proj_far, own_input, peer_input) if step == 0 else ()
        mixed_near, beside = collect(mixed, levels, count, beside)
        if step == 0:
            near_routes, far_routes, later_own, later_peer = beside
            select, combine = call(
                functools.partial(table_body, steps, rows, stride),
                "route_tables",
                [((steps, slots, 2 * rows), F32), ((steps, 2 * rows, slots), F32)],
                [SMEM, SMEM],
                (
                    near_routes[:, x_proj.shape[0] :].astype(F32).reshape(-1),
                    far_routes[:, x_proj.shape[0] :].astype(F32).reshape(-1),
                ),
            )
            later = call(
                functools.partial(later_body, steps, stride),
                "later_inputs",
                [((2 * rows, width), F32)] * (steps - 1),
                [VMEM, VMEM],
                (later_own, later_peer),
            )
        mixed_far = partner(mixed_near, stride, count)
        h, own, other = call(
            route_body,
            "route",
            [
                ((2 * rows, width), F32),
                ((slots // 2, width), BF16),
                ((slots // 2, width), BF16),
            ],
            [VMEM] * 5,
            (mixed_near, mixed_far, x, moe_gain, select[step]),
        )
        picked = spread(jnp.concatenate([own, other_core(other)]), levels, count)
        total_slots = slots * (count // 2)
        returned = call(
            functools.partial(expert_body, parts),
            "experts",
            [((total_slots // parts, width), BF16)] * parts,
            [VMEM] * (parts + 3),
            (*picked, held(gate), held(up), held(down)),
        )
        out_near, _ = collect(returned, levels, count)
        summed = total([out_near, partner(out_near, stride, count)]).astype(BF16)
        out_far = other_core(summed[slots // 2 :])
        if last:
            layer_output = call(
                functools.partial(last_body, step, stride),
                "last_output",
                [((steps, rows, width), BF16)],
                [VMEM] * (4 + step),
                (h, summed, out_far, combine[step], *outputs),
            )[0]
        else:
            out, x, normed = call(
                functools.partial(next_body, stride),
                "next_norm",
                [
                    ((rows, width), BF16),
                    ((2 * rows, width), F32),
                    ((2 * rows, width), BF16),
                ],
                [VMEM] * 6,
                (h, summed, out_far, combine[step], later[step], mamba_gain),
            )
            outputs.append(out)
            rows_in = spread(normed, levels, count)
    return (layer_output, state, conv_state)


def solution(mesh):
    in_specs = (
        P(None, ("group", "dp", "expert"), None),
        P(("group", "dp"), None, "expert"),
        P(("group", "dp"), None, "expert"),
        P(("group", "dp")),
        P(),
        P(None, None, "expert"),
        P(None, "expert"),
        P("expert"),
        P(None, "expert"),
        P(None, "expert"),
        P("expert"),
        P(None, "expert"),
        P("expert"),
        P("expert", None),
        P(),
        P(None, ("group", "dp", "expert"), None),
        P(None, ("group", "dp", "expert"), None),
        P("dp", "expert", None),
        P("dp", "expert", None),
        P("dp", "expert", None),
    )
    out_specs = (
        P(None, ("group", "dp", "expert"), None),
        P(("group", "dp"), None, "expert"),
        P(("group", "dp"), None, "expert"),
    )
    return jax.shard_map(
        on_device, mesh=mesh, in_specs=in_specs, out_specs=out_specs, check_vma=False
    )
```
